32 devices in a mesh: dp: 8 (over y, x, core), tensor: 4 (over z).
Axes of the slice: x: 2, y: 2, z: 4, core: 2. Of those that a mesh axis runs over, the one named last changes fastest.
Arguments:
- inputs: bfloat16 [2048, 8192], P('dp', 'tensor'), may hold values from -6 to 6
- output_gradient: bfloat16 [2048, 8192], P('dp', 'tensor'), may hold values from -6 to 6
- frozen_weight: bfloat16 [8192, 8192], P(None, 'tensor'), may hold values from -0.0625 to 0.0625
- shrink_matrix_stack: bfloat16 [8, 8192, 64], P('dp', 'tensor'), may hold values from -0.0625 to 0.0625
- expand_matrix_stack: bfloat16 [8, 64, 8192], P('dp', None, 'tensor'), may hold values from -0.75 to 0.75
- adapter_index_rows: int32 [2048, 1], P('dp'), may hold values from 0 to 7; in each aligned block of 256 rows (0 to 255, 256 to 511, ...) at most 64 rows name the same one
- adapter_slot: int32 [8], replicated, may hold values from 0 to 7, each once
Outputs:
- projected_values: bfloat16 [2048, 8192], P('dp', 'tensor')
- activation_cotangent: bfloat16 [2048, 8192], P('dp', 'tensor')
- shrink_matrix_cotangent: bfloat16 [8, 8192, 64], P('dp', 'tensor')
- expand_matrix_cotangent: bfloat16 [8, 64, 8192], P('dp', None, 'tensor')
The draws below stay inside these ranges and needn't reach their ends.
Inputs may be any that keep to these rules, and one draw needn't show every extreme that they name: `adapter_index_rows`: among the rows of one index of dp no adapter is named more than 64 times, and in some of these blocks one adapter is named exactly 64 times. `adapter_slot`: each slot holds exactly one adapter; the slot s lies with dp index s.
All inputs are finite; a program needn't handle non-finite values.
Results may differ from the reference program's by a relative error of at most 0.022.
Values may be sent and summed in bfloat16 or wider, within the bound.
No kernel may reach another device: no remote copies, remote signals or barrier semaphores. Data moves between devices by JAX's collectives and lax.ppermute only.
A program may use at most 128 MiB of HBM per device.

```python
import math
import jax
import jax.numpy as jnp
import numpy as np
from jax import lax

MODEL_WIDTH = 8192
ADAPTER_RANK = 64
TOK_DEV = 256
TOKENS = 2048
ADAPTER_TOTAL = 8
CAP = 64
N_TENSOR = 4


def level_of(rng, shape, split, smallest, largest):
    gain = 1.0
    for position, parts in split:
        draws = jax.random.uniform(jax.random.fold_in(jax.random.fold_in(rng, 6), position), (parts,), jnp.float32, smallest / len(split), largest / len(split))
        gain = gain * jnp.repeat(jnp.exp(draws), shape[position] // parts).reshape((-1,) + (1,) * (len(shape) - 1 - position))
    return gain


def assign_block(stream_key, own, number, rows, amount, top, reach, skew):
    sequence = jax.random.permutation(stream_key, amount)
    packed, usual = portions_of(amount, rows * top, reach, skew, True), portions_of(amount, rows * top, reach, skew, False)
    places = jnp.arange(amount)

    def named(tallies, turn):
        used = int((tallies > 0).sum())
        fixed = max(1, used // 4)
        passed = fixed + (places - fixed + turn * (used - fixed)) % max(1, amount - fixed)
        return jnp.zeros((amount,), jnp.int32).at[sequence[jnp.where(places < fixed, places, passed)]].set(jnp.asarray(tallies, jnp.int32))

    tallies = jnp.where(number % 4 == 0, named(packed, number // 4), named(usual, number - number // 4 - 1))
    mixed = jax.random.permutation(jax.random.fold_in(own, 3), amount)
    giver, taker = mixed[0:amount // 2 * 2:2], mixed[1:amount // 2 * 2:2]
    margin = jnp.minimum(tallies[giver] - 1, reach - tallies[taker]) // 2
    margin = jnp.where((giver == sequence[0]) | (taker == sequence[0]) | (tallies[taker] == 0), 0, jnp.maximum(margin, 0))
    passed = jax.random.randint(jax.random.fold_in(own, 4), (amount // 2,), 0, 1 << 20) % (margin + 1)
    tallies = tallies.at[giver].add(-passed).at[taker].add(passed)
    items = jnp.searchsorted(jnp.cumsum(tallies), jnp.arange(rows * top), side="right").astype(jnp.int32)
    table = items.reshape(top, rows).T
    table = table[jax.random.permutation(jax.random.fold_in(own, 1), rows)]
    turn = jax.random.randint(jax.random.fold_in(own, 2), (rows, 1), 0, top)
    return jnp.take_along_axis(table, (jnp.arange(top)[None, :] + turn) % top, axis=1)


def portions_of(count, total, most, skew, full):
    portions = [(1 << 20) // math.isqrt(standing ** skew) + 1 for standing in range(1, count + 1)]
    largest = most if full else min(most, max(-(-total // count), total * portions[0] // sum(portions)))
    least = 1 if total - largest >= count - 1 else 0
    counts, rest = [largest] + [least] * (count - 1), total - largest - least * (count - 1)
    while rest > 0:
        free = [i for i in range(1, count) if counts[i] < largest] or [i for i in range(1, count) if counts[i] < most]
        pool, remaining = sum([portions[i] for i in free]), rest
        for i in free:
            more = min(most - counts[i], max(1, remaining * portions[i] // pool), rest)
            counts[i] = counts[i] + more
            rest = rest - more
    return np.array(counts)


def bell_draw(rng, dims, width, limit, split=(), kind=jnp.bfloat16):
    drawn = jax.random.normal(rng, dims, jnp.float32) * width
    if len(split) > 0:
        drawn = level_of(rng, dims, split, -0.22, 0.18) * drawn
    return jnp.clip(drawn, min=-limit, max=limit).astype(kind)


def setup_inputs(seed: int = 0) -> dict:
    streams_of = jax.random.split(jax.random.key(seed), 8)
    inputs = bell_draw(streams_of[0], (TOKENS, MODEL_WIDTH), 1.0, 6.0, ((0, 8), (1, 4)))
    output_gradient = bell_draw(streams_of[1], (TOKENS, MODEL_WIDTH), 1.0, 6.0, ((0, 8), (1, 4)))
    frozen_weight = bell_draw(streams_of[2], (MODEL_WIDTH, MODEL_WIDTH), MODEL_WIDTH ** -0.5, 0.0625, ((1, 4),))
    shrink_matrix_stack = bell_draw(streams_of[3], (ADAPTER_TOTAL, MODEL_WIDTH, ADAPTER_RANK), MODEL_WIDTH ** -0.5, 0.0625, ((0, 8), (1, 4)))
    expand_matrix_stack = bell_draw(streams_of[4], (ADAPTER_TOTAL, ADAPTER_RANK, MODEL_WIDTH), ADAPTER_RANK ** -0.5, 0.75, ((0, 8), (2, 4)))
    adapter_index_rows_keys = jax.random.split(jax.random.fold_in(streams_of[5], 1), TOKENS // TOK_DEV)
    adapter_index_rows_turns = jax.random.permutation(jax.random.fold_in(streams_of[5], 3), TOKENS // TOK_DEV)
    adapter_index_rows = jax.vmap(lambda own, number: assign_block(jax.random.fold_in(streams_of[5], 2), own, number, TOK_DEV, ADAPTER_TOTAL, 1, CAP, 2))(adapter_index_rows_keys, adapter_index_rows_turns).reshape((TOKENS, 1))
    adapter_slot = jax.random.permutation(streams_of[6], ADAPTER_TOTAL).astype(jnp.int32)
    return {"inputs": inputs, "output_gradient": output_gradient, "frozen_weight": frozen_weight, "shrink_matrix_stack": shrink_matrix_stack, "expand_matrix_stack": expand_matrix_stack, "adapter_index_rows": adapter_index_rows, "adapter_slot": adapter_slot}


adapter_scale = 2.0


def reference(inputs, output_gradient, frozen_weight, shrink_matrix_stack, expand_matrix_stack, adapter_index_rows, adapter_slot):
    frozen_output = jnp.dot(inputs, frozen_weight, preferred_element_type=jnp.float32)
    block = MODEL_WIDTH // N_TENSOR
    frozen_backward = jnp.zeros((inputs.shape[0], MODEL_WIDTH), jnp.float32)
    for index in range(N_TENSOR):
        part = lax.dot_general(output_gradient[:, index * block:(index + 1) * block],
                               frozen_weight[:, index * block:(index + 1) * block],
                               (((1,), (1,)), ((), ())), preferred_element_type=jnp.float32)
        rounded = lax.optimization_barrier(part.astype(jnp.bfloat16))
        frozen_backward = frozen_backward + rounded.astype(jnp.float32)
    slot_position = adapter_slot[adapter_index_rows[:, 0]]

    def lone_entry_place(loop_carry, items):
        lowrank_delta_term, lowrank_reverse_pass = loop_carry
        number, down, upper_limit = items
        chosen = (slot_position == number)[:, None]
        reduced_hidden = jnp.dot(inputs, down, preferred_element_type=jnp.float32).astype(jnp.bfloat16)
        reduced_gradient = (adapter_scale * jnp.dot(output_gradient, upper_limit.T, preferred_element_type=jnp.float32)).astype(jnp.bfloat16)
        reduced_hidden = jnp.where(chosen, reduced_hidden, jnp.zeros_like(reduced_hidden))
        reduced_gradient = jnp.where(chosen, reduced_gradient, jnp.zeros_like(reduced_gradient))
        contribution = (adapter_scale * jnp.dot(reduced_hidden, upper_limit, preferred_element_type=jnp.float32)).astype(jnp.bfloat16)
        backward_result = jnp.dot(reduced_gradient, down.T, preferred_element_type=jnp.float32).astype(jnp.bfloat16)
        up_gradient_piece = (adapter_scale * jnp.dot(reduced_hidden.T, output_gradient, preferred_element_type=jnp.float32)).astype(jnp.bfloat16)
        down_gradient_piece = jnp.dot(inputs.T, reduced_gradient, preferred_element_type=jnp.float32).astype(jnp.bfloat16)
        return (lowrank_delta_term + contribution.astype(jnp.float32), lowrank_reverse_pass + backward_result.astype(jnp.float32)), (down_gradient_piece, up_gradient_piece)

    start_shift = (jnp.zeros((inputs.shape[0], MODEL_WIDTH), jnp.float32), jnp.zeros((inputs.shape[0], MODEL_WIDTH), jnp.float32))
    whole_number_run = jnp.arange(shrink_matrix_stack.shape[0], dtype=jnp.int32)
    (lowrank_delta_term, lowrank_reverse_pass), (shrink_matrix_cotangent, expand_matrix_cotangent) = lax.scan(lone_entry_place, start_shift, (whole_number_run, shrink_matrix_stack, expand_matrix_stack))
    projected_values = (frozen_output + lowrank_delta_term).astype(jnp.bfloat16)
    activation_cotangent = (frozen_backward + lowrank_reverse_pass).astype(jnp.bfloat16)
    return projected_values, activation_cotangent, shrink_matrix_cotangent, expand_matrix_cotangent
```

```python
import jax
import jax.numpy as jnp
from jax import lax
from jax.sharding import PartitionSpec as P

adapter_scale = 2.0
f32, bf16 = jnp.float32, jnp.bfloat16


def dot(a, b, ca, cb):
    return lax.dot_general(a, b, (((ca,), (cb,)), ((), ())), preferred_element_type=f32)


def exchange(x, axis, offset):
    size = lax.axis_size(axis)
    return lax.ppermute(x, axis, [(i, i ^ offset) for i in range(size)])


def body(X, dY, W, A, B, adapter_rows, adapter_slot):
    rows, width = X.shape
    rank = A.shape[2]
    n, D = lax.axis_size("tensor"), lax.axis_size("dp")
    z, me = lax.axis_index("tensor"), lax.axis_index("dp")
    half = D // 2

    own = jnp.concatenate([A[0].T, B[0]], axis=0)
    evens = [own] + [exchange(own, "dp", 2 * j) for j in range(1, half)]
    even = jnp.concatenate([e[:rank] for e in evens] + [e[rank:] for e in evens], axis=0)
    odd = exchange(even, "dp", 1)
    wide = half * rank

    right = [(i, i + 1) for i in range(n - 1)]
    left = [(i + 1, i) for i in range(n - 1)]
    from_left, from_right = [X], [X]
    for s in range(1, n):
        from_left.append(lax.ppermute(from_left[-1], "tensor", right))
        from_right.append(lax.ppermute(from_right[-1], "tensor", left))

    back = dot(dY, W, 1, 1).astype(bf16)
    base_back = lax.psum_scatter(back, "tensor", scatter_dimension=1, tiled=True)

    names = jnp.arange(adapter_slot.shape[0], dtype=jnp.int32)
    slot = jnp.sum(jnp.where(adapter_rows == names[None, :], adapter_slot[None, :], 0), axis=1, keepdims=True)
    offset = slot ^ me
    place = (offset >> 1) + (offset & 1) * half
    group = jnp.arange(D * rank, dtype=jnp.int32) // rank
    chosen = place == group[None, :]
    spread = (jnp.arange(D * rank)[None, :] % rank == jnp.arange(rank)[:, None]).astype(bf16)

    def pick(e, o):
        both = jnp.concatenate([e, o], axis=1)
        return dot(jnp.where(chosen, both, 0).astype(bf16), spread, 1, 1).astype(bf16)

    low_part = pick(dot(X, even[:wide], 1, 1), dot(X, odd[:wide], 1, 1))
    grad_part = pick(dot(dY, even[wide:], 1, 1), dot(dY, odd[wide:], 1, 1))
    part = jnp.concatenate([low_part, grad_part], axis=1)
    total = part.astype(f32)
    for k in range(1, n):
        total = total + exchange(part, "tensor", k).astype(f32)
    low = total[:, :rank].astype(bf16)
    low_grad = (adapter_scale * total[:, rank:]).astype(bf16)
    low_all = jnp.where(chosen, dot(low, spread, 1, 0), 0).astype(bf16)
    grad_all = jnp.where(chosen, dot(low_grad, spread, 1, 0), 0).astype(bf16)

    def grads(part):
        shrink = dot(grad_all[:, part], X, 0, 0)
        expand = adapter_scale * dot(low_all[:, part], dY, 0, 0)
        return jnp.concatenate([shrink, expand], axis=0).astype(bf16)

    there = exchange(grads(slice(wide, 2 * wide)), "dp", 1)
    here = grads(slice(0, wide)).astype(f32) + there.astype(f32)
    blocks = [
        jnp.concatenate([here[j * rank : (j + 1) * rank], here[wide + j * rank : wide + (j + 1) * rank]], axis=0)
        for j in range(half)
    ]
    mine = blocks[0]
    for j in range(1, half):
        mine = mine + exchange(blocks[j].astype(bf16), "dp", 2 * j).astype(f32)
    mine = mine.astype(bf16)

    lora_term = (adapter_scale * (dot(low_all[:, :wide], even[wide:], 1, 0) + dot(low_all[:, wide:], odd[wide:], 1, 0))).astype(bf16)
    lora_back = (dot(grad_all[:, :wide], even[:wide], 1, 0) + dot(grad_all[:, wide:], odd[:wide], 1, 0)).astype(bf16)

    base = dot(X, lax.dynamic_slice(W, (z * width, 0), (width, W.shape[1])), 1, 0)
    for s in range(1, n):
        block = jnp.where(z >= s, from_left[s], from_right[n - s])
        source = lax.rem(z - s + n, n)
        base = base + dot(block, lax.dynamic_slice(W, (source * width, 0), (width, W.shape[1])), 1, 0)

    projected = (base + lora_term.astype(f32)).astype(bf16)
    activation = (base_back.astype(f32) + lora_back.astype(f32)).astype(bf16)
    return projected, activation, mine[:rank].T[None], mine[rank:][None]


def solution(mesh):
    return jax.shard_map(
        body,
        mesh=mesh,
        in_specs=(
            P("dp", "tensor"),
            P("dp", "tensor"),
            P(None, "tensor"),
            P("dp", "tensor", None),
            P("dp", None, "tensor"),
            P("dp", None),
            P(),
        ),
        out_specs=(
            P("dp", "tensor"),
            P("dp", "tensor"),
            P("dp", "tensor", None),
            P("dp", None, "tensor"),
        ),
        check_vma=False,
    )
```

```python
import jax
import jax.numpy as jnp
from jax import lax
from jax.experimental import pallas as pl
from jax.experimental.pallas import tpu as pltpu
from jax.sharding import PartitionSpec as P

adapter_scale = 2.0
f32, bf16 = jnp.float32, jnp.bfloat16
HBM = pl.BlockSpec(memory_space=pltpu.HBM)
LATE = 10**9


def dot(a, b, ca, cb):
    return lax.dot_general(a, b, (((ca,), (cb,)), ((), ())), preferred_element_type=f32)


def exchange(x, axis, offset):
    size = lax.axis_size(axis)
    return lax.ppermute(x, axis, [(i, i ^ offset) for i in range(size)])


def swap(x, axis, groups):
    return lax.all_to_all(x, axis, 0, 0, axis_index_groups=groups, tiled=True)


def after(x, *earlier):
    return lax.optimization_barrier((x,) + earlier)[0]


def call(kernel, grid, prefetch, ins, outs, shapes, scratch, mib=20, cost=1):
    return pl.pallas_call(
        kernel,
        grid_spec=pltpu.PrefetchScalarGridSpec(
            num_scalar_prefetch=prefetch, grid=grid, in_specs=ins, out_specs=outs, scratch_shapes=list(scratch)
        ),
        out_shape=shapes,
        cost_estimate=pl.CostEstimate(flops=cost * 1000, bytes_accessed=cost, transcendentals=0),
        compiler_params=pltpu.CompilerParams(vmem_limit_bytes=mib * 2**20),
    )


def array(*shape):
    return pltpu.HBM(shape, bf16)


def far(*xs):
    return [pltpu.with_memory_space_constraint(x, pltpu.HBM) for x in xs]


def vmem(*shape):
    return pltpu.VMEM(shape, bf16)


def sems(count):
    return pltpu.SemaphoreType.DMA((count,))


def fetch(copies, sem, first=0):
    copies = [pltpu.make_async_copy(a, b, sem.at[first + i]) for i, (a, b) in enumerate(copies)]
    for c in copies:
        c.start()
    return copies


def wait(copies):
    for c in copies:
        c.wait()


def own_adapter(A, B, half):
    rank, width = B.shape

    def kernel(A, B, out, both, sem):
        wait(fetch([(A, both.at[pl.ds(0, rank)]), (B, both.at[pl.ds(rank, rank)])], sem))
        wait(fetch([(both, out.at[j]) for j in range(half)], sem, 2))

    return call(
        kernel, (1,), 0, [HBM, HBM], HBM, array(half, 2 * rank, width), [vmem(2 * rank, width), sems(2 + half)], mib=4
    )(*far(A, B))


def backward(dY, W, n):
    rows, width = dY.shape
    size = W.shape[0] // n

    def kernel(dY, W, out, y, block, sem, out_sem):
        i = pl.program_id(0)
        slot = lax.rem(i, 2)

        def leave(step, slot):
            return pltpu.make_async_copy(block.at[slot], out.at[step], out_sem.at[slot])

        @pl.when(i == 0)
        def _():
            wait(fetch([(dY, y)], sem))

        @pl.when(i >= 2)
        def _():
            leave(i - 2, slot).wait()

        block[slot] = dot(y[...], W[...], 1, 1).astype(bf16)
        leave(i, slot).start()

        @pl.when(i == n - 1)
        def _():
            if n > 1:
                leave(i - 1, 1 - slot).wait()
            leave(i, slot).wait()

    return call(
        kernel,
        (n,),
        0,
        [HBM, pl.BlockSpec((size, width), lambda i: (i, 0))],
        HBM,
        array(n, rows, size),
        [vmem(rows, width), vmem(2, rows, size), sems(1), sems(2)],
        mib=32,
    )(*far(dY, W))


def add_on(plan, at, arrived, back, cost):
    rows, width = arrived.shape
    steps = 4
    size = rows // steps

    def kernel(plan, arrived, back, out, a, b, sem):
        parts = [pl.ds(i * size, size) for i in range(steps)]
        add = plan[at + 1] == 1
        ins = [pltpu.make_async_copy(arrived.at[p], a.at[p], sem.at[i]) for i, p in enumerate(parts)]
        adds = [pltpu.make_async_copy(back.at[plan[at], p], b.at[p], sem.at[steps + i]) for i, p in enumerate(parts)]
        outs = [pltpu.make_async_copy(a.at[p], out.at[p], sem.at[2 * steps + i]) for i, p in enumerate(parts)]
        for i in range(steps):
            ins[i].start()
            pl.when(add)(adds[i].start)
        for i, p in enumerate(parts):
            ins[i].wait()

            @pl.when(add)
            def _():
                adds[i].wait()
                a[p] = (a[p].astype(f32) + b[p].astype(f32)).astype(bf16)

            outs[i].start()
        wait(outs)

    return call(
        kernel,
        (1,),
        1,
        [HBM, HBM],
        HBM,
        array(rows, width),
        [vmem(rows, width), vmem(rows, width), sems(3 * steps)],
        mib=8,
        cost=cost,
    )(plan, *far(arrived, back))


def finish(plan, arrived, back, own, other):
    rows, width = own.shape
    steps = 4
    size = rows // steps

    def kernel(plan, one, two, back, own, other, out, held, done, sem):
        refs = [one, two, back.at[plan[0]], own, other.at[pl.ds(rows, rows)]]
        parts = [pl.ds(i * size, size) for i in range(steps)]
        ins = [
            fetch([(r.at[p], held.at[k, p]) for k, r in enumerate(refs)], sem, i * len(refs))
            for i, p in enumerate(parts)
        ]
        outs = []
        for i, p in enumerate(parts):
            wait(ins[i])
            one, two, base, own, other = (held[k, p].astype(f32) for k in range(len(refs)))
            done[p] = ((one + two + base) + (own + other)).astype(bf16)
            outs += fetch([(done.at[p], out.at[p])], sem, steps * len(refs) + i)
        wait(outs)

    return call(
        kernel,
        (1,),
        1,
        [HBM] * 5,
        HBM,
        array(rows, width),
        [vmem(5, rows, width), vmem(rows, width), sems(6 * steps)],
        mib=16,
    )(plan, *far(arrived[0], arrived[1], back, own, other))


def forward(plan, at, n, W, blocks, term, other):
    rows, width = blocks[0].shape
    columns = W.shape[1]
    split = 2 if columns % 256 == 0 else 1
    part = columns // split

    def kernel(plan, *refs):
        blocks, (W, term, other, out, held, total, terms, sem) = refs[:-8], refs[-8:]
        own, ones, others = blocks[0], blocks[1:n], blocks[n:]
        h, s = pl.program_id(0), pl.program_id(1)

        def copy(ref, i):
            return pltpu.make_async_copy(ref, held.at[i], sem.at[i])

        lora = [
            pltpu.make_async_copy(term, terms.at[0], sem.at[n]),
            pltpu.make_async_copy(other.at[pl.ds(0, rows)], terms.at[1], sem.at[n + 1]),
        ]

        @pl.when((h == 0) & (s == 0))
        def _():
            copy(own, 0).start()
            for i in range(1, n):
                pl.when(plan[at + n + i] == 1)(copy(ones[i - 1], i).start)
                pl.when(plan[at + n + i] == 0)(copy(others[i - 1], i).start)
            for c in lora:
                c.start()

        for i in range(n):
            pl.when((h == 0) & (s == i))(copy(own, i).wait)

        product = jnp.dot(held[s], W[...], preferred_element_type=f32)

        @pl.when(s == 0)
        def _():
            total[...] = product

        @pl.when((s > 0) & (s < n - 1))
        def _():
            total[...] += product

        @pl.when((h == 0) & (s == n - 1))
        def _():
            wait(lora)

        for i in range(split):

            @pl.when((h == i) & (s == n - 1))
            def _():
                mine = slice(i * part, (i + 1) * part)
                added = terms[0, :, mine].astype(f32) + terms[1, :, mine].astype(f32)
                out[...] = (total[...] + product + added).astype(bf16)

    return call(
        kernel,
        (split, n),
        1,
        [HBM] * len(blocks) + [pl.BlockSpec((width, part), lambda h, s, plan: (plan[at + s], h)), HBM, HBM],
        pl.BlockSpec((rows, part), lambda h, s, plan: (0, h)),
        array(rows, columns),
        [vmem(n, rows, width), pltpu.VMEM((rows, part), f32), vmem(2, rows, columns), sems(n + 2)],
        mib=32,
    )(plan, *far(*blocks, W, term, other))


def chosen_of(plan, slots, ids, rank, half):
    slot = jnp.zeros(ids.shape, jnp.int32)
    for a in range(slots.shape[0]):
        slot = jnp.where(ids == a, slots[a], slot)
    column = lax.broadcasted_iota(jnp.int32, (ids.shape[0], half * rank), 1) // rank
    return slot == 2 * column + (plan[1] & 1)


def pieces(gathered, downs, ups, rank):
    half = gathered.shape[0]
    return [(gathered.at[j, pl.ds(0, rank)], downs.at[pl.ds(j * rank, rank)]) for j in range(half)] + [
        (gathered.at[j, pl.ds(rank, rank)], ups.at[pl.ds(j * rank, rank)]) for j in range(half)
    ]


def low_parts(plan, slots, ids, Xs, dYs, gathered, rank, n):
    rows, width = Xs[0].shape
    half = gathered.shape[0]

    def kernel(plan, slots, ids, X, X_other, dY, dY_other, gathered, out, x, y, downs, ups, part, sem):
        top, bottom = pl.ds(0, rows), pl.ds(rows, rows)
        adapters = pieces(gathered, downs, ups, rank)
        ins = fetch([(X, x.at[top]), (X_other, x.at[bottom])] + adapters[:half], sem)
        more = fetch([(dY, y.at[top]), (dY_other, y.at[bottom])] + adapters[half:], sem, 2 + half)
        chosen = chosen_of(plan, slots, ids[...], rank, half)

        def pick(a, b):
            both = jnp.where(chosen, dot(a[...], b[...], 1, 1), 0)
            return sum(both[:, j * rank : (j + 1) * rank] for j in range(half))

        wait(ins)
        low = pick(x, downs)
        wait(more)
        part[...] = jnp.concatenate([low, pick(y, ups)], axis=1).astype(bf16)
        wait(fetch([(part, out.at[k]) for k in range(n)], sem, 4 + 2 * half))

    return call(
        kernel,
        (1,),
        2,
        [pl.BlockSpec((2 * rows, 1), lambda i, *_: (0, 0))] + [HBM] * 5,
        HBM,
        array(n, 2 * rows, 2 * rank),
        [vmem(2 * rows, width)] * 2
        + [vmem(half * rank, width)] * 2
        + [vmem(2 * rows, 2 * rank), sems(4 + 2 * half + n)],
    )(plan, slots, ids, *far(*Xs, *dYs, gathered))


def spread(parts, chosen, rank, half):
    total = sum(parts[k].astype(f32) for k in range(parts.shape[0]))
    low, grad = total[:, :rank].astype(bf16), (adapter_scale * total[:, rank:]).astype(bf16)
    zero = jnp.zeros((), bf16)
    return [jnp.where(chosen, jnp.concatenate([v] * half, axis=1), zero) for v in (low, grad)]


def adapter_grads(plan, slots, ids, parts, Xs, dYs, rank, half):
    rows, width = Xs[0].shape

    def kernel(plan, slots, ids, parts, X, X_other, dY, dY_other, out, held, x, y, grads, sem):
        top, bottom = pl.ds(0, rows), pl.ds(rows, rows)
        ins = fetch(
            [(parts, held), (X, x.at[top]), (X_other, x.at[bottom]), (dY, y.at[top]), (dY_other, y.at[bottom])], sem
        )
        chosen = chosen_of(plan, slots, ids[...], rank, half)
        ins[0].wait()
        low, grad = spread(held, chosen, rank, half)
        wait(ins[1:3])
        shrink = dot(grad, x[...], 0, 0).astype(bf16)
        for j in range(half):
            grads[j, :rank] = shrink[j * rank : (j + 1) * rank]
        wait(ins[3:])
        expand = (adapter_scale * dot(low, y[...], 0, 0)).astype(bf16)
        for j in range(half):
            grads[j, rank:] = expand[j * rank : (j + 1) * rank]
        wait(fetch([(grads, out)], sem, 5))

    return call(
        kernel,
        (1,),
        2,
        [pl.BlockSpec((2 * rows, 1), lambda i, *_: (0, 0))] + [HBM] * 5,
        HBM,
        array(half, 2 * rank, width),
        [vmem(*parts.shape)] + [vmem(2 * rows, width)] * 2 + [vmem(half, 2 * rank, width), sems(6)],
    )(plan, slots, ids, *far(parts, *Xs, *dYs))


def lora_terms(plan, slots, ids, parts, gathered, rank):
    half, width = gathered.shape[0], gathered.shape[2]
    rows = ids.shape[0] // 2

    def kernel(plan, slots, ids, parts, gathered, term, back, other, held, downs, ups, terms, sem):
        ins = fetch([(parts, held)] + pieces(gathered, downs, ups, rank), sem)
        chosen = chosen_of(plan, slots, ids[...], rank, half)
        ins[0].wait()
        low, grad = spread(held, chosen, rank, half)
        wait(ins[1:])
        top, bottom = pl.ds(0, rows), pl.ds(rows, rows)
        terms[0] = (adapter_scale * dot(low, ups[...], 1, 0)).astype(bf16)
        outs = fetch([(terms.at[0, top], term), (terms.at[0, bottom], other.at[top])], sem, 1 + 2 * half)
        terms[1] = dot(grad, downs[...], 1, 0).astype(bf16)
        wait(outs + fetch([(terms.at[1, top], back), (terms.at[1, bottom], other.at[bottom])], sem, 3 + 2 * half))

    return call(
        kernel,
        (1,),
        2,
        [pl.BlockSpec((2 * rows, 1), lambda i, *_: (0, 0)), HBM, HBM],
        [HBM] * 3,
        [array(rows, width), array(rows, width), array(2 * rows, width)],
        [vmem(*parts.shape)] + [vmem(half * rank, width)] * 2 + [vmem(2, 2 * rows, width), sems(5 + 2 * half)],
    )(plan, slots, ids, *far(parts, gathered))


def add_up(blocks, rank):
    half, _, width = blocks.shape

    def kernel(blocks, shrink, expand, held, total, sem):
        wait(fetch([(blocks, held)], sem))
        total[...] = sum(held[j].astype(f32) for j in range(half)).astype(bf16)
        wait(fetch([(total.at[pl.ds(0, rank)], shrink), (total.at[pl.ds(rank, rank)], expand)], sem, 1))

    return call(
        kernel,
        (1,),
        0,
        [HBM],
        [HBM] * 2,
        [array(rank, width)] * 2,
        [vmem(*blocks.shape), vmem(2 * rank, width), sems(3)],
        mib=8,
    )(*far(blocks))


def body(X, dY, W, A, B, adapter_rows, adapter_slot):
    rows, width = X.shape
    rank = A.shape[2]
    n, D = lax.axis_size("tensor"), lax.axis_size("dp")
    z, me = lax.axis_index("tensor"), lax.axis_index("dp")
    half = D // 2
    chips = [list(range(k, D, 2)) for k in (0, 1)]

    odd = me & 1
    place = [jnp.where(odd == 0, z, n - 1 - z), jnp.where(odd == 0, n - 1 - z, z)]
    up = [(d * n + i, d * n + i + 1) for d in range(D) for i in range(n - 1)]
    pairs = [[(a, b) if (a // n) % 2 == k else (b, a) for a, b in up] for k in (0, 1)]

    def along(x, k):
        return lax.ppermute(x, ("dp", "tensor"), pairs[k])

    def z_of(position, k):
        return jnp.where(odd == k, position, n - 1 - position)

    plan = [z, me]
    for s in range(1, n):
        for k in (0, 1):
            plan += [jnp.clip(z_of(n - s + place[k], k), 0, n - 1), place[k] < s]
    plan += [z_of(lax.rem(place[0] - s + n, n), 0) for s in range(n)] + [place[0] >= s for s in range(n)]
    plan = jnp.stack([v.astype(jnp.int32) for v in plan])

    arrived = [[X], [X]]
    arrived[0].append(along(X, 0))

    X_other, dY_other, rows_other = (exchange(v, "dp", 1) for v in (X, dY, adapter_rows))
    others = (X_other, dY_other, rows_other)
    own = own_adapter(A[0].T, after(B, *others)[0], half)
    gathered = swap(own, "dp", chips)
    arrived[1].append(along(after(X, *others), 1))

    ids = jnp.concatenate([adapter_rows, rows_other], axis=0)
    back = backward(after(dY, own, ids), W, n)

    def onward(s, k, *earlier):
        cost = 1 if s < n - 1 else LATE
        payload = add_on(plan, 2 + 4 * (s - 1) + 2 * k, after(arrived[k][s], *earlier), back, cost)
        arrived[k].append(along(payload, k))
        return payload

    payload = onward(1, 0)
    payload = onward(1, 1, payload)

    gathered = after(gathered, payload)
    part = low_parts(plan, adapter_slot, ids, (X, X_other), (dY, dY_other), gathered, rank, n)
    parts = swap(part, "tensor", None)

    payload = onward(2, 0, part)
    payload = onward(2, 1, payload)

    parts = after(parts, payload)
    mine = adapter_grads(plan, adapter_slot, ids, parts, (X, X_other), (dY, dY_other), rank, half)
    arriving = swap(mine, "dp", chips)
    term, back_term, send = lora_terms(plan, adapter_slot, ids, after(parts, mine), gathered, rank)
    other = exchange(send, "dp", 1)

    for s in range(3, n):
        payload = onward(s, 0, payload, send)
        payload = onward(s, 1, payload, send)

    blocks = [after(X, payload)] + arrived[0][1:n] + [arrived[1][n - s] for s in range(1, n)]
    projected = forward(plan, 2 + 4 * (n - 1), n, W, blocks, term, other)

    shrink, expand = add_up(after(arriving, projected), rank)
    activation = finish(plan, (arrived[0][n], arrived[1][n]), back, after(back_term, expand), other)
    return projected, activation, shrink.T[None], expand[None]


def solution(mesh):
    return jax.shard_map(
        body,
        mesh=mesh,
        in_specs=(
            P("dp", "tensor"),
            P("dp", "tensor"),
            P(None, "tensor"),
            P("dp", "tensor", None),
            P("dp", None, "tensor"),
            P("dp", None),
            P(),
        ),
        out_specs=(
            P("dp", "tensor"),
            P("dp", "tensor"),
            P("dp", "tensor", None),
            P("dp", None, "tensor"),
        ),
        check_vma=False,
    )
```

```python
import jax
import jax.numpy as jnp
from jax import lax
from jax.experimental import pallas as pl
from jax.experimental.pallas import tpu as pltpu
from jax.sharding import PartitionSpec as P

adapter_scale = 2.0
f32, bf16 = jnp.float32, jnp.bfloat16
HBM = pl.BlockSpec(memory_space=pltpu.HBM)
LATE = 10**12
GRADS = 10**10
BIG = 63
BACK = 10**10


def dot(a, b, ca, cb):
    return lax.dot_general(a, b, (((ca,), (cb,)), ((), ())), preferred_element_type=f32)


def exchange(x, axis, offset):
    size = lax.axis_size(axis)
    return lax.ppermute(x, axis, [(i, i ^ offset) for i in range(size)])


def swap(x, axis, groups):
    return lax.all_to_all(x, axis, 0, 0, axis_index_groups=groups, tiled=True)


def after(x, *earlier):
    return lax.optimization_barrier((x,) + earlier)[0]


def call(kernel, grid, prefetch, ins, outs, shapes, scratch, mib=BIG, cost=10**3):
    return pl.pallas_call(
        kernel,
        grid_spec=pltpu.PrefetchScalarGridSpec(
            num_scalar_prefetch=prefetch, grid=grid, in_specs=ins, out_specs=outs, scratch_shapes=list(scratch)
        ),
        out_shape=shapes,
        cost_estimate=pl.CostEstimate(flops=cost, bytes_accessed=1, transcendentals=0),
        compiler_params=pltpu.CompilerParams(vmem_limit_bytes=mib * 2**20),
    )


def array(*shape):
    return pltpu.HBM(shape, bf16)


def far(*xs):
    return [pltpu.with_memory_space_constraint(x, pltpu.HBM) for x in xs]


def vmem(*shape):
    return pltpu.VMEM(shape, bf16)


def sems(count):
    return pltpu.SemaphoreType.DMA((count,))


def fetch(copies, sem, first=0):
    copies = [pltpu.make_async_copy(a, b, sem.at[first + i]) for i, (a, b) in enumerate(copies)]
    for c in copies:
        c.start()
    return copies


def wait(copies):
    for c in copies:
        c.wait()


def own_adapter(A, B, half):
    rank, width = B.shape

    def kernel(A, B, out, both, sem):
        wait(fetch([(A, both.at[pl.ds(0, rank)]), (B, both.at[pl.ds(rank, rank)])], sem))
        wait(fetch([(both, out.at[j]) for j in range(half)], sem, 2))

    return call(
        kernel, (1,), 0, [HBM, HBM], HBM, array(half, 2 * rank, width), [vmem(2 * rank, width), sems(2 + half)], mib=4
    )(*far(A, B))


def backward(plan, at, blocks, dY, W, n, cost):
    rows, width = dY.shape
    size = W.shape[0] // n
    fine = 4 if size % 512 == 0 else 1
    coarse = 2 if fine == 4 else 1
    tile, chunk = size // coarse, size // fine

    def kernel(plan, dY, W, out, y, w, done, sem, out_sem):
        ins = fetch([(dY, y)], sem)
        for b in range(blocks):
            for i in range(fine):
                source = pl.multiple_of(plan[at + b] * size + i * chunk, chunk)
                to = pl.ds(b * size + i * chunk, chunk)
                ins += fetch([(W.at[pl.ds(source, chunk)], w.at[to])], sem, 1 + b * fine + i)
        ins[0].wait()
        outs = []
        for b in range(blocks):
            for i in range(coarse):
                per = fine // coarse
                first = 1 + b * fine + i * per
                wait(ins[first : first + per])
                span = pl.ds(i * tile, tile)
                done[b, :, span] = dot(y[...], w[pl.ds(b * size + i * tile, tile)], 1, 1).astype(bf16)
                outs += fetch([(done.at[b, :, span], out.at[b, :, span])], out_sem, b * coarse + i)
        wait(outs)

    return call(
        kernel,
        (1,),
        1,
        [HBM, HBM],
        HBM,
        array(blocks, rows, size),
        [
            vmem(rows, width),
            vmem(blocks * size, width),
            vmem(blocks, rows, size),
            sems(1 + blocks * fine),
            sems(blocks * coarse),
        ],
        mib=BIG,
        cost=cost,
    )(plan, *far(dY, W))


def add_on(plan, at, arrived, backs, cost):
    rows, width = arrived.shape
    steps = 4
    size = rows // steps
    count = backs[0].shape[0]

    def kernel(plan, arrived, *refs):
        backs, (out, a, b, sem) = refs[: len(backs_)], refs[len(backs_) :]
        parts = [pl.ds(i * size, size) for i in range(steps)]
        add = plan[at + 1] == 1
        ins = [pltpu.make_async_copy(arrived.at[p], a.at[p], sem.at[i]) for i, p in enumerate(parts)]
        adds = [
            [pltpu.make_async_copy(r.at[lax.rem(plan[at], count), p], b.at[p], sem.at[steps + i]) for r in backs]
            for i, p in enumerate(parts)
        ]
        outs = [pltpu.make_async_copy(a.at[p], out.at[p], sem.at[2 * steps + i]) for i, p in enumerate(parts)]
        for i in range(steps):
            ins[i].start()
            for k in range(len(backs)):
                pl.when(add & (lax.div(plan[at], count) == k))(adds[i][k].start)
        for i, p in enumerate(parts):
            ins[i].wait()

            @pl.when(add)
            def _():
                adds[i][0].wait()
                a[p] = (a[p].astype(f32) + b[p].astype(f32)).astype(bf16)

            outs[i].start()
        wait(outs)

    backs_ = backs
    return call(
        kernel,
        (1,),
        1,
        [HBM] * (1 + len(backs)),
        HBM,
        array(rows, width),
        [vmem(rows, width), vmem(rows, width), sems(3 * steps)],
        mib=8,
        cost=cost,
    )(plan, *far(arrived, *backs))


def finish(plan, arrived, back, own, other):
    rows, width = own.shape
    steps = 4
    size = rows // steps

    def kernel(plan, one, two, back, own, other, out, held, done, sem):
        refs = [one, two, back.at[back.shape[0] - 1], own, other.at[pl.ds(rows, rows)]]
        parts = [pl.ds(i * size, size) for i in range(steps)]
        ins = [
            fetch([(r.at[p], held.at[k, p]) for k, r in enumerate(refs)], sem, i * len(refs))
            for i, p in enumerate(parts)
        ]
        outs = []
        for i, p in enumerate(parts):
            wait(ins[i])
            one, two, base, own, other = (held[k, p].astype(f32) for k in range(len(refs)))
            done[p] = ((one + two + base) + (own + other)).astype(bf16)
            outs += fetch([(done.at[p], out.at[p])], sem, steps * len(refs) + i)
        wait(outs)

    return call(
        kernel,
        (1,),
        1,
        [HBM] * 5,
        HBM,
        array(rows, width),
        [vmem(5, rows, width), vmem(rows, width), sems(6 * steps)],
        mib=16,
    )(plan, *far(arrived[0], arrived[1], back, own, other))


def forward(plan, at, n, W, blocks, rest=()):
    rows, width = blocks[0][0].shape
    columns = W.shape[1]
    fine = 4 if width % 512 == 0 else 1
    coarse = 2 if fine == 4 else 1
    tile, chunk = width // coarse, width // fine
    count = len(blocks)
    arrays = [b for block in blocks for b in block]

    def kernel(plan, *refs):
        flat, W, rest_ = refs[: len(arrays)], refs[len(arrays)], refs[len(arrays) + 1 : len(arrays) + 1 + len(rest)]
        out, held, w, total, *sides, sem, side_sem = refs[len(arrays) + 1 + len(rest) :]
        flat = iter(flat)
        mine = [[next(flat) for _ in block] for block in blocks]
        ins, lefts = [], []
        for s, block in enumerate(mine):
            pick = [pltpu.make_async_copy(ref, held.at[s], side_sem.at[s]) for ref in block]
            if len(block) == 1:
                pick[0].start()
            else:
                pl.when(plan[at + 2 * s + 1] == 1)(pick[0].start)
                pl.when(plan[at + 2 * s + 1] == 0)(pick[1].start)
            lefts.append(pick[0])
            for i in range(fine):
                source = pl.multiple_of(plan[at + 2 * s] * width + i * chunk, chunk)
                to = pl.ds(s * width + i * chunk, chunk)
                ins += fetch([(W.at[pl.ds(source, chunk)], w.at[to])], sem, s * fine + i)
        added = []
        if rest:
            pairs = [(rest_[0], sides[0]), (rest_[1], sides[1].at[0]), (rest_[2].at[pl.ds(0, rows)], sides[1].at[1])]
            added = fetch(pairs, side_sem, count)
        for s in range(count):
            lefts[s].wait()
            for i in range(coarse):
                per = fine // coarse
                wait(ins[s * fine + i * per : s * fine + (i + 1) * per])
                span = pl.ds(i * tile, tile)
                product = dot(held[s, :, span], w[pl.ds(s * width + i * tile, tile)], 1, 0)
                if s + i == 0:
                    total[...] = product
                else:
                    total[...] += product
        wait(added)
        if rest:
            lora = sides[1][0].astype(f32) + sides[1][1].astype(f32)
            sides[2][...] = (total[...] + sides[0][...] + lora).astype(bf16)
            wait(fetch([(sides[2], out)], side_sem, count + 3))
        else:
            wait(fetch([(total, out)], side_sem, count + 3))

    scratch = [vmem(count, rows, width), vmem(count * width, columns), pltpu.VMEM((rows, columns), f32)]
    if rest:
        scratch += [pltpu.VMEM((rows, columns), f32), vmem(2, rows, columns), vmem(rows, columns)]
    return call(
        kernel,
        (1,),
        1,
        [HBM] * (len(arrays) + 1 + len(rest)),
        HBM,
        pltpu.HBM((rows, columns), bf16 if rest else f32),
        scratch + [sems(count * fine), sems(count + 4)],
        mib=BIG,
    )(plan, *far(*arrays, W, *rest))


def chosen_of(plan, slots, ids, rank, half):
    slot = jnp.zeros(ids.shape, jnp.int32)
    for a in range(slots.shape[0]):
        slot = jnp.where(ids == a, slots[a], slot)
    column = lax.broadcasted_iota(jnp.int32, (ids.shape[0], half * rank), 1) // rank
    return slot == 2 * column + plan[0]


def pieces(gathered, downs, ups, rank):
    half = gathered.shape[0]
    return [(gathered.at[j, pl.ds(0, rank)], downs.at[pl.ds(j * rank, rank)]) for j in range(half)] + [
        (gathered.at[j, pl.ds(rank, rank)], ups.at[pl.ds(j * rank, rank)]) for j in range(half)
    ]


def low_parts(plan, slots, ids, Xs, dYs, gathered, rank, n):
    rows, width = Xs[0].shape
    half = gathered.shape[0]

    def kernel(plan, slots, ids, X, X_other, dY, dY_other, gathered, out, x, y, downs, ups, part, sem):
        top, bottom = pl.ds(0, rows), pl.ds(rows, rows)
        adapters = pieces(gathered, downs, ups, rank)
        ins = fetch([(X, x.at[top]), (X_other, x.at[bottom])] + adapters[:half], sem)
        more = fetch([(dY, y.at[top]), (dY_other, y.at[bottom])] + adapters[half:], sem, 2 + half)
        chosen = chosen_of(plan, slots, ids[...], rank, half)

        def pick(a, b):
            both = jnp.where(chosen, dot(a[...], b[...], 1, 1), 0)
            return sum(both[:, j * rank : (j + 1) * rank] for j in range(half))

        wait(ins)
        low = pick(x, downs)
        wait(more)
        part[...] = jnp.concatenate([low, pick(y, ups)], axis=1).astype(bf16)
        wait(fetch([(part, out.at[k]) for k in range(n)], sem, 4 + 2 * half))

    return call(
        kernel,
        (1,),
        2,
        [pl.BlockSpec((2 * rows, 1), lambda i, *_: (0, 0))] + [HBM] * 5,
        HBM,
        array(n, 2 * rows, 2 * rank),
        [vmem(2 * rows, width)] * 2
        + [vmem(half * rank, width)] * 2
        + [vmem(2 * rows, 2 * rank), sems(4 + 2 * half + n)],
    )(plan, slots, ids, *far(*Xs, *dYs, gathered))


def spread(parts, chosen, rank, half):
    total = sum(parts[k].astype(f32) for k in range(parts.shape[0]))
    low, grad = total[:, :rank].astype(bf16), (adapter_scale * total[:, rank:]).astype(bf16)
    zero = jnp.zeros((), bf16)
    return [jnp.where(chosen, jnp.concatenate([v] * half, axis=1), zero) for v in (low, grad)]


def adapter_grads(plan, slots, ids, parts, Xs, dYs, rank, half):
    rows, width = Xs[0].shape

    def kernel(plan, slots, ids, parts, X, X_other, dY, dY_other, out, held, x, y, grads, sem):
        top, bottom = pl.ds(0, rows), pl.ds(rows, rows)
        ins = fetch(
            [(parts, held), (X, x.at[top]), (X_other, x.at[bottom]), (dY, y.at[top]), (dY_other, y.at[bottom])], sem
        )
        chosen = chosen_of(plan, slots, ids[...], rank, half)
        ins[0].wait()
        low, grad = spread(held, chosen, rank, half)
        wait(ins[1:3])
        shrink = dot(grad, x[...], 0, 0).astype(bf16)
        for j in range(half):
            grads[j, :rank] = shrink[j * rank : (j + 1) * rank]
        wait(ins[3:])
        expand = (adapter_scale * dot(low, y[...], 0, 0)).astype(bf16)
        for j in range(half):
            grads[j, rank:] = expand[j * rank : (j + 1) * rank]
        wait(fetch([(grads, out)], sem, 5))

    return call(
        kernel,
        (1,),
        2,
        [pl.BlockSpec((2 * rows, 1), lambda i, *_: (0, 0))] + [HBM] * 5,
        HBM,
        array(half, 2 * rank, width),
        [vmem(*parts.shape)] + [vmem(2 * rows, width)] * 2 + [vmem(half, 2 * rank, width), sems(6)],
        cost=GRADS,
    )(plan, slots, ids, *far(parts, *Xs, *dYs))


def lora_terms(plan, slots, ids, parts, gathered, rank):
    half, width = gathered.shape[0], gathered.shape[2]
    rows = ids.shape[0] // 2

    def kernel(plan, slots, ids, parts, gathered, term, back, other, held, downs, ups, terms, sem):
        ins = fetch([(parts, held)] + pieces(gathered, downs, ups, rank), sem)
        chosen = chosen_of(plan, slots, ids[...], rank, half)
        ins[0].wait()
        low, grad = spread(held, chosen, rank, half)
        wait(ins[1:])
        top, bottom = pl.ds(0, rows), pl.ds(rows, rows)
        terms[0] = (adapter_scale * dot(low, ups[...], 1, 0)).astype(bf16)
        outs = fetch([(terms.at[0, top], term), (terms.at[0, bottom], other.at[top])], sem, 1 + 2 * half)
        terms[1] = dot(grad, downs[...], 1, 0).astype(bf16)
        wait(outs + fetch([(terms.at[1, top], back), (terms.at[1, bottom], other.at[bottom])], sem, 3 + 2 * half))

    return call(
        kernel,
        (1,),
        2,
        [pl.BlockSpec((2 * rows, 1), lambda i, *_: (0, 0)), HBM, HBM],
        [HBM] * 3,
        [array(rows, width), array(rows, width), array(2 * rows, width)],
        [vmem(*parts.shape)] + [vmem(half * rank, width)] * 2 + [vmem(2, 2 * rows, width), sems(5 + 2 * half)],
    )(plan, slots, ids, *far(parts, gathered))


def add_up(blocks, rank):
    half, _, width = blocks.shape

    def kernel(blocks, shrink, expand, held, total, sem):
        wait(fetch([(blocks, held)], sem))
        total[...] = sum(held[j].astype(f32) for j in range(half)).astype(bf16)
        wait(fetch([(total.at[pl.ds(0, rank)], shrink), (total.at[pl.ds(rank, rank)], expand)], sem, 1))

    return call(
        kernel,
        (1,),
        0,
        [HBM],
        [HBM] * 2,
        [array(rank, width)] * 2,
        [vmem(*blocks.shape), vmem(2 * rank, width), sems(3)],
        mib=8,
    )(*far(blocks))


def body(X, dY, W, A, B, adapter_rows, adapter_slot):
    rows, width = X.shape
    rank = A.shape[2]
    n, D = lax.axis_size("tensor"), lax.axis_size("dp")
    z, me = lax.axis_index("tensor"), lax.axis_index("dp")
    half = D // 2
    chips = [list(range(k, D, 2)) for k in (0, 1)]

    odd = me & 1
    up = [(d * n + i, d * n + i + 1) for d in range(D) for i in range(n - 1)]
    pairs = [[(a, b) if (a // n) % 2 == k else (b, a) for a, b in up] for k in (0, 1)]

    def along(x, k):
        return lax.ppermute(x, ("dp", "tensor"), pairs[k])

    early = [s for s in range(1, n) if 2 * s == n] + [0]
    late = [s for s in range(1, n) if 2 * s != n]
    table = []
    for i in range(n):
        for k in (0, 1):
            order = sorted(range(n), key=lambda d: (-abs(d - i), d))
            row = [k] + order
            for s in range(1, n):
                for way in (0, 1):
                    p = i if k == way else n - 1 - i
                    target = min(max(n - s + p, 0), n - 1)
                    row += [order.index(target if k == way else n - 1 - target), int(p < s)]
            p = i if k == 0 else n - 1 - i
            for s in early + late:
                source = (p - s) % n
                row += [source if k == 0 else n - 1 - source, int(p >= s)]
            table.append(row)
    steps_at, forward_at = 1 + n, 1 + n + 4 * (n - 1)
    plan = lax.dynamic_index_in_dim(jnp.asarray(table, jnp.int32), 2 * z + odd, 0, keepdims=False)

    arrived = [[X], [X]]
    arrived[0].append(along(X, 0))

    X_other, dY_other, rows_other = (exchange(v, "dp", 1) for v in (X, dY, adapter_rows))
    others = (X_other, dY_other, rows_other)
    own = own_adapter(A[0].T, after(B, *others)[0], half)
    gathered = swap(own, "dp", chips)
    arrived[1].append(along(after(X, *others), 1))

    ids = jnp.concatenate([adapter_rows, rows_other], axis=0)
    first = n // 2
    backs = [backward(plan, 1, first, after(dY, own, ids), W, n, 10**3)]

    def onward(s, k, last):
        cost = 10**3 if s < n - 1 else LATE
        payload = add_on(plan, steps_at + 4 * (s - 1) + 2 * k, after(arrived[k][s], last), backs, cost)
        arrived[k].append(along(payload, k))
        return payload

    last = onward(1, 0, backs[0])
    last = onward(1, 1, last)
    backs.append(backward(plan, 1 + first, n - first, after(dY, last), W, n, BACK))

    gathered = after(gathered, backs[1])
    part = low_parts(plan, adapter_slot, ids, (X, X_other), (dY, dY_other), gathered, rank, n)
    parts = swap(part, "tensor", None)

    def block(s):
        return (arrived[0][s], arrived[1][n - s]) if s else (X,)

    last = part
    for s in range(2, n):
        last = onward(s, 0, last)
        if s == n // 2:
            begun = forward(plan, forward_at, n, W, [block(s) for s in early[:-1]] + [(after(X, last),)])
            last = begun
        if s == 3:
            term, back_term, send = lora_terms(plan, adapter_slot, ids, after(parts, last), gathered, rank)
            other = exchange(send, "dp", 1)
            last = send
        last = onward(s, 1, last)
        if s == 2:
            parts = after(parts, last)
            mine = adapter_grads(plan, adapter_slot, ids, parts, (X, X_other), (dY, dY_other), rank, half)
            arriving = swap(mine, "dp", chips)
            last = mine

    rest = (after(begun, last), term, other)
    projected = forward(plan, forward_at + 2 * len(early), n, W, [block(s) for s in late], rest)

    shrink, expand = add_up(after(arriving, projected), rank)
    activation = finish(plan, (arrived[0][n], arrived[1][n]), backs[1], after(back_term, expand), other)
    return projected, activation, shrink.T[None], expand[None]


def solution(mesh):
    return jax.shard_map(
        body,
        mesh=mesh,
        in_specs=(
            P("dp", "tensor"),
            P("dp", "tensor"),
            P(None, "tensor"),
            P("dp", "tensor", None),
            P("dp", None, "tensor"),
            P("dp", None),
            P(),
        ),
        out_specs=(
            P("dp", "tensor"),
            P("dp", "tensor"),
            P("dp", "tensor", None),
            P("dp", None, "tensor"),
        ),
        check_vma=False,
    )
```

```python
import jax
import jax.numpy as jnp
from jax import lax
from jax.experimental import pallas as pl
from jax.experimental.pallas import tpu as pltpu
from jax.sharding import PartitionSpec as P

adapter_scale = 2.0
f32, bf16 = jnp.float32, jnp.bfloat16
HBM = pl.BlockSpec(memory_space=pltpu.HBM)
LATE = 10**12
GRADS = 10**10
BIG = 63
SOON = 10**10
AHEAD = 3


def dot(a, b, ca, cb):
    return lax.dot_general(a, b, (((ca,), (cb,)), ((), ())), preferred_element_type=f32)


def exchange(x, axis, offset):
    size = lax.axis_size(axis)
    return lax.ppermute(x, axis, [(i, i ^ offset) for i in range(size)])


def swap(x, axis, groups):
    return lax.all_to_all(x, axis, 0, 0, axis_index_groups=groups, tiled=True)


def after(x, *earlier):
    return lax.optimization_barrier((x,) + earlier)[0]


def call(kernel, grid, prefetch, ins, outs, shapes, scratch, mib=BIG, cost=10**3):
    return pl.pallas_call(
        kernel,
        grid_spec=pltpu.PrefetchScalarGridSpec(
            num_scalar_prefetch=prefetch, grid=grid, in_specs=ins, out_specs=outs, scratch_shapes=list(scratch)
        ),
        out_shape=shapes,
        cost_estimate=pl.CostEstimate(flops=cost, bytes_accessed=1, transcendentals=0),
        compiler_params=pltpu.CompilerParams(vmem_limit_bytes=mib * 2**20),
    )


def array(*shape):
    return pltpu.HBM(shape, bf16)


def far(*xs):
    return [pltpu.with_memory_space_constraint(x, pltpu.HBM) for x in xs]


def vmem(*shape):
    return pltpu.VMEM(shape, bf16)


def look_up(spot, table, column):
    value = jnp.int32(table[0][column])
    for i, row in enumerate(table[1:], 1):
        value = jnp.where(spot[0] == i, row[column], value)
    return value


def sems(count):
    return pltpu.SemaphoreType.DMA((count,))


def fetch(copies, sem, first=0):
    copies = [pltpu.make_async_copy(a, b, sem.at[first + i]) for i, (a, b) in enumerate(copies)]
    for c in copies:
        c.start()
    return copies


def wait(copies):
    for c in copies:
        c.wait()


def own_adapter(A, B, half):
    rank, width = B.shape

    def kernel(A, B, out, both, sem):
        wait(fetch([(A, both.at[pl.ds(0, rank)]), (B, both.at[pl.ds(rank, rank)])], sem))
        wait(fetch([(both, out.at[j]) for j in range(half)], sem, 2))

    return call(
        kernel, (1,), 0, [HBM, HBM], HBM, array(half, 2 * rank, width), [vmem(2 * rank, width), sems(2 + half)], mib=4
    )(*far(A, B))


class Stream:
    def __init__(self, W, w, starts, size, sem):
        chunk = size // 4 if size % 512 == 0 else size
        self.copies, self.started, self.done = [], 0, 0
        for b, start in enumerate(starts):
            for i in range(size // chunk):
                source = W.at[pl.ds(pl.multiple_of(start * size + i * chunk, chunk), chunk)]
                k = len(self.copies)
                self.copies.append(pltpu.make_async_copy(source, w.at[pl.ds(b * size + i * chunk, chunk)], sem.at[k]))

    def start(self, count):
        for c in self.copies[self.started : self.started + count]:
            c.start()
        self.started += count

    def take(self, parts):
        for _ in range(len(self.copies) // parts):
            self.copies[self.done].wait()
            self.done += 1
            self.start(1)


def backward_blocks(y, w, done, out, stream, size, sem):
    blocks = done.shape[0]
    coarse = 2 if size % 512 == 0 else 1
    tile = size // coarse
    outs = []
    for b in range(blocks):
        for i in range(coarse):
            stream.take(blocks * coarse)
            span = pl.ds(i * tile, tile)
            done[b, :, span] = dot(y, w[pl.ds(b * size + i * tile, tile)], 1, 1).astype(bf16)
            outs += fetch([(done.at[b, :, span], out.at[b, :, span])], sem, b * coarse + i)
    return outs


def backward(spot, table, columns, dY, W, n):
    rows, width = dY.shape
    size = W.shape[0] // n
    blocks = len(columns)

    def kernel(spot, dY, W, out, y, w, done, sem, out_sem, y_sem):
        ready = fetch([(dY, y)], y_sem)
        ins = Stream(W, w, [look_up(spot, table, c) for c in columns], size, sem)
        ins.start(AHEAD)
        wait(ready)
        wait(backward_blocks(y[...], w, done, out, ins, size, out_sem))

    return call(
        kernel,
        (1,),
        1,
        [HBM, HBM],
        HBM,
        array(blocks, rows, size),
        [vmem(rows, width), vmem(blocks * size, width), vmem(blocks, rows, size), sems(4 * blocks), sems(2 * blocks), sems(1)],
    )(spot, *far(dY, W))


def add_on(spot, table, at, arrived, backs, cost):
    rows, width = arrived.shape
    steps = 4
    size = rows // steps
    count = backs[0].shape[0]

    def kernel(spot, arrived, *refs):
        backs, (out, a, b, sem) = refs[:-4], refs[-4:]
        parts = [pl.ds(i * size, size) for i in range(steps)]
        add, block = look_up(spot, table, at + 1) == 1, look_up(spot, table, at)
        ins = [pltpu.make_async_copy(arrived.at[p], a.at[p], sem.at[i]) for i, p in enumerate(parts)]
        adds = [
            [pltpu.make_async_copy(r.at[lax.rem(block, count), p], b.at[p], sem.at[steps + i]) for r in backs]
            for i, p in enumerate(parts)
        ]
        outs = [pltpu.make_async_copy(a.at[p], out.at[p], sem.at[2 * steps + i]) for i, p in enumerate(parts)]
        for i in range(steps):
            ins[i].start()
            for k in range(len(backs)):
                pl.when(add & (lax.div(block, count) == k))(adds[i][k].start)
        for i, p in enumerate(parts):
            ins[i].wait()

            @pl.when(add)
            def _():
                adds[i][0].wait()
                a[p] = (a[p].astype(f32) + b[p].astype(f32)).astype(bf16)

            outs[i].start()
        wait(outs)

    return call(
        kernel,
        (1,),
        1,
        [HBM] * (1 + len(backs)),
        HBM,
        array(rows, width),
        [vmem(rows, width), vmem(rows, width), sems(3 * steps)],
        mib=8,
        cost=cost,
    )(spot, *far(arrived, *backs))


def finish(arrived, rest, blocks, rank):
    rows, width = rest.shape
    half = blocks.shape[0]
    steps = 4
    size = rows // steps

    def kernel(one, two, rest, blocks, out, shrink, expand, held, done, parts, total, sem, more):
        refs = [one, two, rest]
        spans = [pl.ds(i * size, size) for i in range(steps)]
        ins = [
            fetch([(r.at[p], held.at[k, p]) for k, r in enumerate(refs)], sem, i * len(refs))
            for i, p in enumerate(spans)
        ]
        gradients = fetch([(blocks, parts)], more)
        outs = []
        for i, p in enumerate(spans):
            wait(ins[i])
            done[p] = (held[0, p].astype(f32) + held[1, p].astype(f32) + held[2, p].astype(f32)).astype(bf16)
            outs += fetch([(done.at[p], out.at[p])], sem, steps * len(refs) + i)
        wait(gradients)
        total[...] = sum(parts[j].astype(f32) for j in range(half)).astype(bf16)
        outs += fetch([(total.at[pl.ds(0, rank)], shrink), (total.at[pl.ds(rank, rank)], expand)], more, 1)
        wait(outs)

    return call(
        kernel,
        (1,),
        0,
        [HBM] * 4,
        [HBM] * 3,
        [array(rows, width), array(rank, width), array(rank, width)],
        [vmem(3, rows, width), vmem(rows, width), vmem(*blocks.shape), vmem(2 * rank, width), sems(4 * steps), sems(3)],
        mib=16,
    )(*far(*arrived, rest, blocks))


def forward(spot, table, at, n, W, blocks, terms, back):
    rows, width = blocks[0][0].shape
    columns = W.shape[1]
    coarse = 2 if width % 512 == 0 else 1
    tile = width // coarse
    count = len(blocks)
    arrays = [b for block in blocks for b in block]

    def kernel(spot, *refs):
        flat, (W, term, back_term, other, back) = refs[: len(arrays)], refs[len(arrays) : len(arrays) + 5]
        out, rest, held, w, total, sides, sem, side_sem = refs[len(arrays) + 5 :]
        flat = iter(flat)
        mine = [[next(flat) for _ in block] for block in blocks]
        lefts = []
        for s, block in enumerate(mine):
            pick = [pltpu.make_async_copy(ref, held.at[s], side_sem.at[s]) for ref in block]
            if len(block) == 1:
                pick[0].start()
            else:
                one = look_up(spot, table, at + 2 * s + 1) == 1
                pl.when(one)(pick[0].start)
                pl.when(jnp.logical_not(one))(pick[1].start)
            lefts.append(pick[0])
        ins = Stream(W, w, [look_up(spot, table, at + 2 * s) for s in range(count)], width, sem)
        ins.start(AHEAD)
        own, theirs = pl.ds(0, rows), pl.ds(rows, rows)
        pairs = [term, other.at[own], back_term, other.at[theirs], back.at[back.shape[0] - 1]]
        for s in range(count):
            lefts[s].wait()
            for i in range(coarse):
                k = s * coarse + i
                ins.take(count * coarse)
                if k == count * coarse // 2:
                    added = fetch([(r, sides.at[i]) for i, r in enumerate(pairs)], side_sem, count)
                product = dot(held[s, :, pl.ds(i * tile, tile)], w[pl.ds(s * width + i * tile, tile)], 1, 0)
                if k == 0:
                    total[...] = product
                else:
                    total[...] += product
        wait(added)
        sides[0] = (total[...] + (sides[0].astype(f32) + sides[1].astype(f32))).astype(bf16)
        outs = fetch([(sides.at[0], out)], side_sem, count + 5)
        sides[2] = (sides[2].astype(f32) + sides[3].astype(f32) + sides[4].astype(f32)).astype(bf16)
        wait(outs + fetch([(sides.at[2], rest)], side_sem, count + 6))

    return call(
        kernel,
        (1,),
        1,
        [HBM] * (len(arrays) + 5),
        [HBM] * 2,
        [array(rows, columns), array(rows, width)],
        [
            vmem(count, rows, width),
            vmem(count * width, columns),
            pltpu.VMEM((rows, columns), f32),
            vmem(5, rows, columns),
            sems(4 * count),
            sems(count + 7),
        ],
    )(spot, *far(*arrays, W, *terms, back))


def chosen_of(spot, slots, ids, rank, half):
    ids = jnp.concatenate([r[...] for r in ids], axis=1)
    slot = jnp.zeros(ids.shape, jnp.int32)
    for a in range(slots.shape[0]):
        slot = jnp.where(ids == a, slots[a], slot)
    column = lax.broadcasted_iota(jnp.int32, (half * rank, ids.shape[1]), 0) // rank
    return jnp.where(slot == 2 * column + lax.rem(spot[0], 2), 1.0, 0.0).T > 0.5


def pieces(gathered, downs, ups, rank):
    half = gathered.shape[0]
    return [(gathered.at[j, pl.ds(0, rank)], downs.at[pl.ds(j * rank, rank)]) for j in range(half)] + [
        (gathered.at[j, pl.ds(rank, rank)], ups.at[pl.ds(j * rank, rank)]) for j in range(half)
    ]


def rows_of(X, dY, x, y, rows):
    top, bottom = pl.ds(0, rows), pl.ds(rows, rows)
    return [(X[0], x.at[top]), (X[1], x.at[bottom]), (dY[0], y.at[top]), (dY[1], y.at[bottom])]


def ids_spec(rows):
    return pl.BlockSpec((1, rows), lambda i, *_: (0, 0))


def low_parts(spot, slots, ids, Xs, dYs, gathered, rank, n):
    rows, width = Xs[0].shape
    half = gathered.shape[0]

    def kernel(spot, slots, id0, id1, X, X_other, dY, dY_other, gathered, out, x, y, downs, ups, part, sem):
        rights = pieces(gathered, downs, ups, rank)
        lefts = rows_of((X, X_other), (dY, dY_other), x, y, rows)
        ready = fetch(lefts[:2] + rights[:half], sem)
        more = fetch(lefts[2:] + rights[half:], sem, 2 + half)
        chosen = chosen_of(spot, slots, (id0, id1), rank, half)

        def pick(a, b):
            both = jnp.where(chosen, dot(a[...], b[...], 1, 1), 0)
            return sum(both[:, j * rank : (j + 1) * rank] for j in range(half))

        wait(ready)
        low = pick(x, downs)
        wait(more)
        part[...] = jnp.concatenate([low, pick(y, ups)], axis=1).astype(bf16)
        wait(fetch([(part, out.at[k]) for k in range(n)], sem, 4 + 2 * half))

    return call(
        kernel,
        (1,),
        2,
        [ids_spec(rows)] * 2 + [HBM] * 5,
        HBM,
        array(n, 2 * rows, 2 * rank),
        [vmem(2 * rows, width)] * 2
        + [vmem(half * rank, width)] * 2
        + [vmem(2 * rows, 2 * rank), sems(4 + 2 * half + n)],
    )(spot, slots, *ids, *far(*Xs, *dYs, gathered))


def adapters(spot, slots, ids, parts, Xs, dYs, gathered, rank):
    rows, width = Xs[0].shape
    half = gathered.shape[0]

    def kernel(spot, slots, id0, id1, parts, X, X_other, dY, dY_other, gathered, out, term, back, other, *scratch):
        held, x, y, downs, ups, grads, terms, sem, out_sem = scratch
        ins = fetch(
            [(parts, held)] + rows_of((X, X_other), (dY, dY_other), x, y, rows) + pieces(gathered, downs, ups, rank), sem
        )
        chosen = chosen_of(spot, slots, (id0, id1), rank, half)
        ins[0].wait()
        total = sum(held[k].astype(f32) for k in range(held.shape[0]))
        low, grad = total[:, :rank].astype(bf16), (adapter_scale * total[:, rank:]).astype(bf16)
        zero = jnp.zeros((), bf16)
        low, grad = [jnp.where(chosen, jnp.concatenate([v] * half, axis=1), zero) for v in (low, grad)]
        wait(ins[1:3])
        shrink = dot(grad, x[...], 0, 0).astype(bf16)
        for j in range(half):
            grads[j, :rank] = shrink[j * rank : (j + 1) * rank]
        wait(ins[3:5])
        expand = (adapter_scale * dot(low, y[...], 0, 0)).astype(bf16)
        for j in range(half):
            grads[j, rank:] = expand[j * rank : (j + 1) * rank]
        outs = fetch([(grads, out)], out_sem)
        wait(ins[5:])
        top, bottom = pl.ds(0, rows), pl.ds(rows, rows)
        terms[0] = (adapter_scale * dot(low, ups[...], 1, 0)).astype(bf16)
        outs += fetch([(terms.at[0, top], term), (terms.at[0, bottom], other.at[top])], out_sem, 1)
        terms[1] = dot(grad, downs[...], 1, 0).astype(bf16)
        outs += fetch([(terms.at[1, top], back), (terms.at[1, bottom], other.at[bottom])], out_sem, 3)
        wait(outs)

    return call(
        kernel,
        (1,),
        2,
        [ids_spec(rows)] * 2 + [HBM] * 6,
        [HBM] * 4,
        [array(half, 2 * rank, width), array(rows, width), array(rows, width), array(2 * rows, width)],
        [vmem(*parts.shape)]
        + [vmem(2 * rows, width)] * 2
        + [vmem(half * rank, width)] * 2
        + [vmem(half, 2 * rank, width), vmem(2, 2 * rows, width), sems(5 + 2 * half), sems(5)],
        cost=GRADS,
    )(spot, slots, *ids, *far(parts, *Xs, *dYs, gathered))


def body(X, dY, W, A, B, adapter_rows, adapter_slot):
    rows, width = X.shape
    rank = A.shape[2]
    n, D = lax.axis_size("tensor"), lax.axis_size("dp")
    z, me = lax.axis_index("tensor"), lax.axis_index("dp")
    half = D // 2
    chips = [list(range(k, D, 2)) for k in (0, 1)]

    odd = me & 1
    up = [(d * n + i, d * n + i + 1) for d in range(D) for i in range(n - 1)]
    pairs = [[(a, b) if (a // n) % 2 == k else (b, a) for a, b in up] for k in (0, 1)]

    def along(x, k):
        return lax.ppermute(x, ("dp", "tensor"), pairs[k])

    table = []
    for i in range(n):
        for k in (0, 1):
            order = sorted(range(n), key=lambda d: (-abs(d - i), d))
            row = [k] + order
            for s in range(1, n):
                for way in (0, 1):
                    p = i if k == way else n - 1 - i
                    target = min(max(n - s + p, 0), n - 1)
                    row += [order.index(target if k == way else n - 1 - target), int(p < s)]
            p = i if k == 0 else n - 1 - i
            for s in range(n):
                source = (p - s) % n
                row += [source if k == 0 else n - 1 - source, int(p >= s)]
            table.append(row)
    steps_at, forward_at = 1 + n, 1 + n + 4 * (n - 1)
    spot = jnp.stack([2 * z + odd])

    arrived = [[X], [X]]
    arrived[0].append(along(X, 0))

    X_other, dY_other, rows_other = (exchange(v, "dp", 1) for v in (X, dY, adapter_rows))
    others = (X_other, dY_other, rows_other)
    own = own_adapter(A[0].T, after(B, *others)[0], half)
    gathered = swap(own, "dp", chips)
    arrived[1].append(along(after(X, own), 1))

    first, second = list(range(1, n)), [n]
    backs = [backward(spot, table, first, after(dY, own, *others), W, n)]

    def onward(s, k, last):
        cost = LATE if s == n - 1 else SOON if (s, k) == (1, 1) else 10**3
        payload = add_on(spot, table, steps_at + 4 * (s - 1) + 2 * k, after(arrived[k][s], last), backs, cost)
        arrived[k].append(along(payload, k))
        return payload

    last = onward(1, 0, backs[0])
    last = onward(1, 1, last)

    ids = adapter_rows.reshape(1, rows), rows_other.reshape(1, rows)
    Xs, dYs = (X, X_other), (dY, dY_other)
    gathered = after(gathered, last)
    part = low_parts(spot, adapter_slot, ids, Xs, dYs, gathered, rank, n)
    parts = swap(part, "tensor", None)

    last = part
    for s in range(2, n):
        last = onward(s, 0, last)
        if s == 2:
            own_back = backward(spot, table, second, after(dY, last), W, n)
            last = own_back
        last = onward(s, 1, last)
        if s == 2:
            parts = after(parts, last)
            mine, term, back_term, send = adapters(spot, adapter_slot, ids, parts, Xs, dYs, gathered, rank)
            arriving = swap(mine, "dp", chips)
            other = exchange(send, "dp", 1)
            last = send

    blocks = [(after(X, last),)] + [(arrived[0][s], arrived[1][n - s]) for s in range(1, n)]
    projected, rest = forward(spot, table, forward_at, n, W, blocks, (term, back_term, other), own_back)
    activation, shrink, expand = finish((arrived[0][n], arrived[1][n]), rest, arriving, rank)
    return projected, activation, shrink.T[None], expand[None]


def solution(mesh):
    return jax.shard_map(
        body,
        mesh=mesh,
        in_specs=(
            P("dp", "tensor"),
            P("dp", "tensor"),
            P(None, "tensor"),
            P("dp", "tensor", None),
            P("dp", None, "tensor"),
            P("dp", None),
            P(),
        ),
        out_specs=(
            P("dp", "tensor"),
            P("dp", "tensor"),
            P("dp", "tensor", None),
            P("dp", None, "tensor"),
        ),
        check_vma=False,
    )
```

```python
import jax
import jax.numpy as jnp
from jax import lax
from jax.experimental import pallas as pl
from jax.experimental.pallas import tpu as pltpu
from jax.sharding import PartitionSpec as P

adapter_scale = 2.0
f32, bf16 = jnp.float32, jnp.bfloat16
HBM = pl.BlockSpec(memory_space=pltpu.HBM)
LATE = 10**12
GRADS = 10**10
BIG = 63
SOON = 10**10


def dot(a, b, ca, cb):
    return lax.dot_general(a, b, (((ca,), (cb,)), ((), ())), preferred_element_type=f32)


def exchange(x, axis, offset):
    size = lax.axis_size(axis)
    return lax.ppermute(x, axis, [(i, i ^ offset) for i in range(size)])


def swap(x, axis, groups):
    return lax.all_to_all(x, axis, 0, 0, axis_index_groups=groups, tiled=True)


def after(x, *earlier):
    return lax.optimization_barrier((x,) + earlier)[0]


def call(kernel, grid, prefetch, ins, outs, shapes, scratch, mib=BIG, cost=10**3):
    return pl.pallas_call(
        kernel,
        grid_spec=pltpu.PrefetchScalarGridSpec(
            num_scalar_prefetch=prefetch, grid=grid, in_specs=ins, out_specs=outs, scratch_shapes=list(scratch)
        ),
        out_shape=shapes,
        cost_estimate=pl.CostEstimate(flops=cost, bytes_accessed=1, transcendentals=0),
        compiler_params=pltpu.CompilerParams(vmem_limit_bytes=mib * 2**20),
    )


def array(*shape):
    return pltpu.HBM(shape, bf16)


def far(*xs):
    return [pltpu.with_memory_space_constraint(x, pltpu.HBM) for x in xs]


def vmem(*shape):
    return pltpu.VMEM(shape, bf16)


def look_up(spot, table, column):
    value = jnp.int32(table[0][column])
    for i, row in enumerate(table[1:], 1):
        value = jnp.where(spot[0] == i, row[column], value)
    return value


def sems(count):
    return pltpu.SemaphoreType.DMA((count,))


def fetch(copies, sem, first=0):
    copies = [pltpu.make_async_copy(a, b, sem.at[first + i]) for i, (a, b) in enumerate(copies)]
    for c in copies:
        c.start()
    return copies


def wait(copies):
    for c in copies:
        c.wait()


def own_adapter(A, B, half):
    rank, width = B.shape

    def kernel(A, B, out, both, sem):
        wait(fetch([(A, both.at[pl.ds(0, rank)]), (B, both.at[pl.ds(rank, rank)])], sem))
        wait(fetch([(both, out.at[j]) for j in range(half)], sem, 2))

    return call(
        kernel, (1,), 0, [HBM, HBM], HBM, array(half, 2 * rank, width), [vmem(2 * rank, width), sems(2 + half)], mib=4
    )(*far(A, B))


class Stream:
    def __init__(self, W, w, starts, size, sem):
        chunk = size // 4 if size % 512 == 0 else size
        self.copies, self.started, self.done = [], 0, 0
        for b, start in enumerate(starts):
            for i in range(size // chunk):
                source = W.at[pl.ds(pl.multiple_of(start * size + i * chunk, chunk), chunk)]
                k = len(self.copies)
                self.copies.append(pltpu.make_async_copy(source, w.at[pl.ds(b * size + i * chunk, chunk)], sem.at[k]))

    def start(self, count):
        for c in self.copies[self.started : self.started + count]:
            c.start()
        self.started += count

    def take(self, parts):
        for _ in range(len(self.copies) // parts):
            self.copies[self.done].wait()
            self.done += 1
            self.start(1)


def backward_blocks(y, w, done, out, stream, size, sem):
    blocks = done.shape[0]
    coarse = 2 if size % 512 == 0 else 1
    tile = size // coarse
    outs = []
    for b in range(blocks):
        for i in range(coarse):
            stream.take(blocks * coarse)
            span = pl.ds(i * tile, tile)
            done[b, :, span] = dot(y, w[pl.ds(b * size + i * tile, tile)], 1, 1).astype(bf16)
            outs += fetch([(done.at[b, :, span], out.at[b, :, span])], sem, b * coarse + i)
    return outs


def backward(spot, table, columns, dY, W, n):
    rows, width = dY.shape
    size = W.shape[0] // n
    blocks = len(columns)

    def kernel(spot, dY, W, out, y, w, done, sem, out_sem, y_sem):
        ready = fetch([(dY, y)], y_sem)
        ins = Stream(W, w, [look_up(spot, table, c) for c in columns], size, sem)
        ins.start(4)
        wait(ready)
        wait(backward_blocks(y[...], w, done, out, ins, size, out_sem))

    return call(
        kernel,
        (1,),
        1,
        [HBM, HBM],
        HBM,
        array(blocks, rows, size),
        [vmem(rows, width), vmem(blocks * size, width), vmem(blocks, rows, size), sems(4 * blocks), sems(2 * blocks), sems(1)],
    )(spot, *far(dY, W))


def add_on(spot, table, at, arrived, backs, cost):
    rows, width = arrived.shape
    steps = 4
    size = rows // steps
    count = backs[0].shape[0]

    def kernel(spot, arrived, *refs):
        backs, (out, a, b, sem) = refs[:-4], refs[-4:]
        parts = [pl.ds(i * size, size) for i in range(steps)]
        add, block = look_up(spot, table, at + 1) == 1, look_up(spot, table, at)
        ins = [pltpu.make_async_copy(arrived.at[p], a.at[p], sem.at[i]) for i, p in enumerate(parts)]
        adds = [
            [pltpu.make_async_copy(r.at[lax.rem(block, count), p], b.at[p], sem.at[steps + i]) for r in backs]
            for i, p in enumerate(parts)
        ]
        outs = [pltpu.make_async_copy(a.at[p], out.at[p], sem.at[2 * steps + i]) for i, p in enumerate(parts)]
        for i in range(steps):
            ins[i].start()
            for k in range(len(backs)):
                pl.when(add & (lax.div(block, count) == k))(adds[i][k].start)
        for i, p in enumerate(parts):
            ins[i].wait()

            @pl.when(add)
            def _():
                adds[i][0].wait()
                a[p] = (a[p].astype(f32) + b[p].astype(f32)).astype(bf16)

            outs[i].start()
        wait(outs)

    return call(
        kernel,
        (1,),
        1,
        [HBM] * (1 + len(backs)),
        HBM,
        array(rows, width),
        [vmem(rows, width), vmem(rows, width), sems(3 * steps)],
        mib=8,
        cost=cost,
    )(spot, *far(arrived, *backs))


def finish(arrived, rest, blocks, rank):
    rows, width = rest.shape
    half = blocks.shape[0]
    steps = 4
    size = rows // steps

    def kernel(one, two, rest, blocks, out, shrink, expand, held, done, parts, total, sem, more):
        refs = [one, two, rest]
        spans = [pl.ds(i * size, size) for i in range(steps)]
        ins = [
            fetch([(r.at[p], held.at[k, p]) for k, r in enumerate(refs)], sem, i * len(refs))
            for i, p in enumerate(spans)
        ]
        gradients = fetch([(blocks, parts)], more)
        outs = []
        for i, p in enumerate(spans):
            wait(ins[i])
            done[p] = (held[0, p].astype(f32) + held[1, p].astype(f32) + held[2, p].astype(f32)).astype(bf16)
            outs += fetch([(done.at[p], out.at[p])], sem, steps * len(refs) + i)
        wait(gradients)
        total[...] = sum(parts[j].astype(f32) for j in range(half)).astype(bf16)
        outs += fetch([(total.at[pl.ds(0, rank)], shrink), (total.at[pl.ds(rank, rank)], expand)], more, 1)
        wait(outs)

    return call(
        kernel,
        (1,),
        0,
        [HBM] * 4,
        [HBM] * 3,
        [array(rows, width), array(rank, width), array(rank, width)],
        [vmem(3, rows, width), vmem(rows, width), vmem(*blocks.shape), vmem(2 * rank, width), sems(4 * steps), sems(3)],
        mib=16,
    )(*far(*arrived, rest, blocks))


def forward(spot, table, at, n, W, blocks, terms, back):
    rows, width = blocks[0][0].shape
    columns = W.shape[1]
    coarse = 2 if width % 512 == 0 else 1
    tile = width // coarse
    count = len(blocks)
    arrays = [b for block in blocks for b in block]

    def kernel(spot, *refs):
        flat, (W, term, back_term, other, back) = refs[: len(arrays)], refs[len(arrays) : len(arrays) + 5]
        out, rest, held, w, total, sides, sem, side_sem = refs[len(arrays) + 5 :]
        flat = iter(flat)
        mine = [[next(flat) for _ in block] for block in blocks]
        lefts = []
        for s, block in enumerate(mine):
            pick = [pltpu.make_async_copy(ref, held.at[s], side_sem.at[s]) for ref in block]
            if len(block) == 1:
                pick[0].start()
            else:
                one = look_up(spot, table, at + 2 * s + 1) == 1
                pl.when(one)(pick[0].start)
                pl.when(jnp.logical_not(one))(pick[1].start)
            lefts.append(pick[0])
        ins = Stream(W, w, [look_up(spot, table, at + 2 * s) for s in range(count)], width, sem)
        ins.start(6)
        own, theirs = pl.ds(0, rows), pl.ds(rows, rows)
        pairs = [term, other.at[own], back_term, other.at[theirs], back.at[back.shape[0] - 1]]
        for s in range(count):
            lefts[s].wait()
            for i in range(coarse):
                k = s * coarse + i
                ins.take(count * coarse)
                if k == count * coarse // 2:
                    added = fetch([(r, sides.at[i]) for i, r in enumerate(pairs)], side_sem, count)
                product = dot(held[s, :, pl.ds(i * tile, tile)], w[pl.ds(s * width + i * tile, tile)], 1, 0)
                if k == 0:
                    total[...] = product
                else:
                    total[...] += product
        wait(added)
        sides[0] = (total[...] + (sides[0].astype(f32) + sides[1].astype(f32))).astype(bf16)
        outs = fetch([(sides.at[0], out)], side_sem, count + 5)
        sides[2] = (sides[2].astype(f32) + sides[3].astype(f32) + sides[4].astype(f32)).astype(bf16)
        wait(outs + fetch([(sides.at[2], rest)], side_sem, count + 6))

    return call(
        kernel,
        (1,),
        1,
        [HBM] * (len(arrays) + 5),
        [HBM] * 2,
        [array(rows, columns), array(rows, width)],
        [
            vmem(count, rows, width),
            vmem(count * width, columns),
            pltpu.VMEM((rows, columns), f32),
            vmem(5, rows, columns),
            sems(4 * count),
            sems(count + 7),
        ],
    )(spot, *far(*arrays, W, *terms, back))


def chosen_of(spot, slots, ids, rank, half):
    ids = jnp.concatenate([r[...] for r in ids], axis=1)
    slot = jnp.zeros(ids.shape, jnp.int32)
    for a in range(slots.shape[0]):
        slot = jnp.where(ids == a, slots[a], slot)
    column = lax.broadcasted_iota(jnp.int32, (half * rank, ids.shape[1]), 0) // rank
    return jnp.where(slot == 2 * column + lax.rem(spot[0], 2), 1.0, 0.0).T > 0.5


def pieces(gathered, downs, ups, rank):
    half = gathered.shape[0]
    return [(gathered.at[j, pl.ds(0, rank)], downs.at[pl.ds(j * rank, rank)]) for j in range(half)] + [
        (gathered.at[j, pl.ds(rank, rank)], ups.at[pl.ds(j * rank, rank)]) for j in range(half)
    ]


def rows_of(X, dY, x, y, rows):
    top, bottom = pl.ds(0, rows), pl.ds(rows, rows)
    return [(X[0], x.at[top]), (X[1], x.at[bottom]), (dY[0], y.at[top]), (dY[1], y.at[bottom])]


def ids_spec(rows):
    return pl.BlockSpec((1, rows), lambda i, *_: (0, 0))


def low_parts(spot, slots, ids, Xs, dYs, gathered, rank, n):
    rows, width = Xs[0].shape
    half = gathered.shape[0]

    def kernel(spot, slots, id0, id1, X, X_other, dY, dY_other, gathered, out, x, y, downs, ups, part, sem):
        rights = pieces(gathered, downs, ups, rank)
        lefts = rows_of((X, X_other), (dY, dY_other), x, y, rows)
        ready = fetch(lefts[:2] + rights[:half], sem)
        more = fetch(lefts[2:] + rights[half:], sem, 2 + half)
        chosen = chosen_of(spot, slots, (id0, id1), rank, half)

        def pick(a, b):
            both = jnp.where(chosen, dot(a[...], b[...], 1, 1), 0)
            return sum(both[:, j * rank : (j + 1) * rank] for j in range(half))

        wait(ready)
        low = pick(x, downs)
        wait(more)
        part[...] = jnp.concatenate([low, pick(y, ups)], axis=1).astype(bf16)
        wait(fetch([(part, out.at[k]) for k in range(n)], sem, 4 + 2 * half))

    return call(
        kernel,
        (1,),
        2,
        [ids_spec(rows)] * 2 + [HBM] * 5,
        HBM,
        array(n, 2 * rows, 2 * rank),
        [vmem(2 * rows, width)] * 2
        + [vmem(half * rank, width)] * 2
        + [vmem(2 * rows, 2 * rank), sems(4 + 2 * half + n)],
    )(spot, slots, *ids, *far(*Xs, *dYs, gathered))


def adapters(spot, slots, ids, parts, Xs, dYs, gathered, rank):
    rows, width = Xs[0].shape
    half = gathered.shape[0]

    def kernel(spot, slots, id0, id1, parts, X, X_other, dY, dY_other, gathered, out, term, back, other, *scratch):
        x, y, downs, ups, grads, terms, sem, out_sem = scratch
        ins = fetch(
            rows_of((X, X_other), (dY, dY_other), x, y, rows) + pieces(gathered, downs, ups, rank), sem
        )
        chosen = chosen_of(spot, slots, (id0, id1), rank, half)
        total = sum(parts[k].astype(f32) for k in range(parts.shape[0]))
        low, grad = total[:, :rank].astype(bf16), (adapter_scale * total[:, rank:]).astype(bf16)
        zero = jnp.zeros((), bf16)
        low, grad = [jnp.where(chosen, jnp.concatenate([v] * half, axis=1), zero) for v in (low, grad)]
        wait(ins[:2])
        shrink = dot(grad, x[...], 0, 0).astype(bf16)
        for j in range(half):
            grads[j, :rank] = shrink[j * rank : (j + 1) * rank]
        wait(ins[2:4])
        expand = (adapter_scale * dot(low, y[...], 0, 0)).astype(bf16)
        for j in range(half):
            grads[j, rank:] = expand[j * rank : (j + 1) * rank]
        outs = fetch([(grads, out)], out_sem)
        wait(ins[4:])
        top, bottom = pl.ds(0, rows), pl.ds(rows, rows)
        terms[0] = (adapter_scale * dot(low, ups[...], 1, 0)).astype(bf16)
        outs += fetch([(terms.at[0, top], term), (terms.at[0, bottom], other.at[top])], out_sem, 1)
        terms[1] = dot(grad, downs[...], 1, 0).astype(bf16)
        outs += fetch([(terms.at[1, top], back), (terms.at[1, bottom], other.at[bottom])], out_sem, 3)
        wait(outs)

    return call(
        kernel,
        (1,),
        2,
        [ids_spec(rows)] * 2 + [pl.BlockSpec(memory_space=pltpu.VMEM)] + [HBM] * 5,
        [HBM] * 4,
        [array(half, 2 * rank, width), array(rows, width), array(rows, width), array(2 * rows, width)],
        [vmem(2 * rows, width)] * 2
        + [vmem(half * rank, width)] * 2
        + [vmem(half, 2 * rank, width), vmem(2, 2 * rows, width), sems(4 + 2 * half), sems(5)],
        mib=60,
        cost=GRADS,
    )(spot, slots, *ids, pltpu.with_memory_space_constraint(parts, pltpu.VMEM), *far(*Xs, *dYs, gathered))


def body(X, dY, W, A, B, adapter_rows, adapter_slot):
    rows, width = X.shape
    rank = A.shape[2]
    n, D = lax.axis_size("tensor"), lax.axis_size("dp")
    z, me = lax.axis_index("tensor"), lax.axis_index("dp")
    half = D // 2
    chips = [list(range(k, D, 2)) for k in (0, 1)]

    odd = me & 1
    up = [(d * n + i, d * n + i + 1) for d in range(D) for i in range(n - 1)]
    pairs = [[(a, b) if (a // n) % 2 == k else (b, a) for a, b in up] for k in (0, 1)]

    def along(x, k):
        return lax.ppermute(x, ("dp", "tensor"), pairs[k])

    table = []
    for i in range(n):
        for k in (0, 1):
            order = sorted(range(n), key=lambda d: (-abs(d - i), d))
            row = [k] + order
            for s in range(1, n):
                for way in (0, 1):
                    p = i if k == way else n - 1 - i
                    target = min(max(n - s + p, 0), n - 1)
                    row += [order.index(target if k == way else n - 1 - target), int(p < s)]
            p = i if k == 0 else n - 1 - i
            for s in range(n):
                source = (p - s) % n
                row += [source if k == 0 else n - 1 - source, int(p >= s)]
            table.append(row)
    steps_at, forward_at = 1 + n, 1 + n + 4 * (n - 1)
    spot = jnp.stack([2 * z + odd])

    arrived = [[X], [X]]
    arrived[0].append(along(X, 0))

    X_other, dY_other, rows_other = (exchange(v, "dp", 1) for v in (X, dY, adapter_rows))
    others = (X_other, dY_other, rows_other)
    own = own_adapter(A[0].T, after(B, *others)[0], half)
    gathered = swap(own, "dp", chips)
    arrived[1].append(along(after(X, own), 1))

    first, second, third = list(range(1, n - 1)), [n - 1], [n]
    backs = [backward(spot, table, first, after(dY, own, *others), W, n)]

    def onward(s, k, last):
        cost = LATE if s == n - 1 else SOON if (s, k) == (1, 1) else 10**3
        payload = add_on(spot, table, steps_at + 4 * (s - 1) + 2 * k, after(arrived[k][s], last), backs, cost)
        arrived[k].append(along(payload, k))
        return payload

    last = onward(1, 0, backs[0])
    last = onward(1, 1, last)

    ids = adapter_rows.reshape(1, rows), rows_other.reshape(1, rows)
    Xs, dYs = (X, X_other), (dY, dY_other)
    backs.append(backward(spot, table, second, after(dY, last), W, n))
    gathered = after(gathered, backs[1])
    part = low_parts(spot, adapter_slot, ids, Xs, dYs, gathered, rank, n)
    parts = swap(part, "tensor", None)

    last = part
    for s in range(2, n):
        last = onward(s, 0, last)
        if s == 2:
            own_back = backward(spot, table, third, after(dY, last), W, n)
            last = own_back
        last = onward(s, 1, last)
        if s == 2:
            parts = after(parts, last)
            mine, term, back_term, send = adapters(spot, adapter_slot, ids, parts, Xs, dYs, gathered, rank)
            arriving = swap(mine, "dp", chips)
            other = exchange(send, "dp", 1)
            last = send

    blocks = [(after(X, last),)] + [(arrived[0][s], arrived[1][n - s]) for s in range(1, n)]
    projected, rest = forward(spot, table, forward_at, n, W, blocks, (term, back_term, other), own_back)
    activation, shrink, expand = finish((arrived[0][n], arrived[1][n]), rest, arriving, rank)
    return projected, activation, shrink.T[None], expand[None]


def solution(mesh):
    return jax.shard_map(
        body,
        mesh=mesh,
        in_specs=(
            P("dp", "tensor"),
            P("dp", "tensor"),
            P(None, "tensor"),
            P("dp", "tensor", None),
            P("dp", None, "tensor"),
            P("dp", None),
            P(),
        ),
        out_specs=(
            P("dp", "tensor"),
            P("dp", "tensor"),
            P("dp", "tensor", None),
            P("dp", None, "tensor"),
        ),
        check_vma=False,
    )
```

```python
import jax
import jax.numpy as jnp
from jax import lax
from jax.experimental import pallas as pl
from jax.experimental.pallas import tpu as pltpu
from jax.sharding import PartitionSpec as P

adapter_scale = 2.0
f32, bf16 = jnp.float32, jnp.bfloat16
HBM = pl.BlockSpec(memory_space=pltpu.HBM)
LATE = 10**12
GRADS = 10**10
BIG = 63
SOON = 10**10


def dot(a, b, ca, cb):
    return lax.dot_general(a, b, (((ca,), (cb,)), ((), ())), preferred_element_type=f32)


def exchange(x, axis, offset):
    size = lax.axis_size(axis)
    return lax.ppermute(x, axis, [(i, i ^ offset) for i in range(size)])


def swap(x, axis, groups):
    return lax.all_to_all(x, axis, 0, 0, axis_index_groups=groups, tiled=True)


def after(x, *earlier):
    return lax.optimization_barrier((x,) + earlier)[0]


def call(kernel, grid, prefetch, ins, outs, shapes, scratch, mib=BIG, cost=10**3):
    return pl.pallas_call(
        kernel,
        grid_spec=pltpu.PrefetchScalarGridSpec(
            num_scalar_prefetch=prefetch, grid=grid, in_specs=ins, out_specs=outs, scratch_shapes=list(scratch)
        ),
        out_shape=shapes,
        cost_estimate=pl.CostEstimate(flops=cost, bytes_accessed=1, transcendentals=0),
        compiler_params=pltpu.CompilerParams(vmem_limit_bytes=mib * 2**20),
    )


def array(*shape):
    return pltpu.HBM(shape, bf16)


def far(*xs):
    return [pltpu.with_memory_space_constraint(x, pltpu.HBM) for x in xs]


def vmem(*shape):
    return pltpu.VMEM(shape, bf16)


def look_up(spot, table, column):
    value = jnp.int32(table[0][column])
    for i, row in enumerate(table[1:], 1):
        value = jnp.where(spot[0] == i, row[column], value)
    return value


def sems(count):
    return pltpu.SemaphoreType.DMA((count,))


def fetch(copies, sem, first=0):
    copies = [pltpu.make_async_copy(a, b, sem.at[first + i]) for i, (a, b) in enumerate(copies)]
    for c in copies:
        c.start()
    return copies


def wait(copies):
    for c in copies:
        c.wait()


def own_adapter(A, B, half):
    rank, width = B.shape

    def kernel(A, B, out, both, sem):
        wait(fetch([(A, both.at[pl.ds(0, rank)]), (B, both.at[pl.ds(rank, rank)])], sem))
        wait(fetch([(both, out.at[j]) for j in range(half)], sem, 2))

    return call(
        kernel, (1,), 0, [HBM, HBM], HBM, array(half, 2 * rank, width), [vmem(2 * rank, width), sems(2 + half)], mib=4
    )(*far(A, B))


class Stream:
    def __init__(self, W, w, starts, size, sem):
        chunk = size // 4 if size % 512 == 0 else size
        self.copies, self.started, self.done = [], 0, 0
        for b, start in enumerate(starts):
            for i in range(size // chunk):
                source = W.at[pl.ds(pl.multiple_of(start * size + i * chunk, chunk), chunk)]
                k = len(self.copies)
                self.copies.append(pltpu.make_async_copy(source, w.at[pl.ds(b * size + i * chunk, chunk)], sem.at[k]))

    def start(self, count):
        for c in self.copies[self.started : self.started + count]:
            c.start()
        self.started += count

    def take(self, parts):
        for _ in range(len(self.copies) // parts):
            self.copies[self.done].wait()
            self.done += 1
            self.start(1)


def backward_blocks(y, w, done, out, stream, size, coarse, sem):
    blocks = done.shape[0]
    tile = size // coarse
    outs = []
    for b in range(blocks):
        for i in range(coarse):
            stream.take(blocks * coarse)
            span = pl.ds(i * tile, tile)
            done[b, :, span] = dot(y, w[pl.ds(b * size + i * tile, tile)], 1, 1).astype(bf16)
            outs += fetch([(done.at[b, :, span], out.at[b, :, span])], sem, b * coarse + i)
    return outs


def backward(spot, table, columns, dY, W, n):
    rows, width = dY.shape
    size = W.shape[0] // n
    blocks = len(columns)
    coarse = 1 if size % 512 else 2 if blocks > 1 else 4

    def kernel(spot, dY, W, out, y, w, done, sem, out_sem, y_sem):
        ready = fetch([(dY, y)], y_sem)
        ins = Stream(W, w, [look_up(spot, table, c) for c in columns], size, sem)
        ins.start(4 if blocks > 1 else 2)
        wait(ready)
        wait(backward_blocks(y[...], w, done, out, ins, size, coarse, out_sem))

    return call(
        kernel,
        (1,),
        1,
        [HBM, HBM],
        HBM,
        array(blocks, rows, size),
        [vmem(rows, width), vmem(blocks * size, width), vmem(blocks, rows, size), sems(4 * blocks), sems(4 * blocks), sems(1)],
    )(spot, *far(dY, W))


def add_on(spot, table, at, arrived, backs, cost):
    rows, width = arrived.shape
    steps = 4
    size = rows // steps
    count = backs[0].shape[0]

    def kernel(spot, arrived, *refs):
        backs, (out, a, b, sem) = refs[:-4], refs[-4:]
        parts = [pl.ds(i * size, size) for i in range(steps)]
        add, block = look_up(spot, table, at + 1) == 1, look_up(spot, table, at)
        ins = [pltpu.make_async_copy(arrived.at[p], a.at[p], sem.at[i]) for i, p in enumerate(parts)]
        adds = [
            [pltpu.make_async_copy(r.at[lax.rem(block, count), p], b.at[p], sem.at[steps + i]) for r in backs]
            for i, p in enumerate(parts)
        ]
        outs = [pltpu.make_async_copy(a.at[p], out.at[p], sem.at[2 * steps + i]) for i, p in enumerate(parts)]
        for i in range(steps):
            ins[i].start()
            for k in range(len(backs)):
                pl.when(add & (lax.div(block, count) == k))(adds[i][k].start)
        for i, p in enumerate(parts):
            ins[i].wait()

            @pl.when(add)
            def _():
                adds[i][0].wait()
                a[p] = (a[p].astype(f32) + b[p].astype(f32)).astype(bf16)

            outs[i].start()
        wait(outs)

    return call(
        kernel,
        (1,),
        1,
        [HBM] * (1 + len(backs)),
        HBM,
        array(rows, width),
        [vmem(rows, width), vmem(rows, width), sems(3 * steps)],
        mib=8,
        cost=cost,
    )(spot, *far(arrived, *backs))


def finish(arrived, rest):
    rows, width = rest.shape
    steps = 4
    size = rows // steps

    def kernel(one, two, rest, out, held, done, sem):
        refs = [one, two, rest]
        spans = [pl.ds(i * size, size) for i in range(steps)]
        ins = [
            fetch([(r.at[p], held.at[k, p]) for k, r in enumerate(refs)], sem, i * len(refs))
            for i, p in enumerate(spans)
        ]
        outs = []
        for i, p in enumerate(spans):
            wait(ins[i])
            done[p] = (held[0, p].astype(f32) + held[1, p].astype(f32) + held[2, p].astype(f32)).astype(bf16)
            outs += fetch([(done.at[p], out.at[p])], sem, steps * len(refs) + i)
        wait(outs)

    return call(
        kernel,
        (1,),
        0,
        [HBM] * 3,
        HBM,
        array(rows, width),
        [vmem(3, rows, width), vmem(rows, width), sems(4 * steps)],
        mib=16,
    )(*far(*arrived, rest))


def add_up(blocks, rank):
    half, _, width = blocks.shape

    def kernel(blocks, shrink, expand, parts, total, sem):
        wait(fetch([(blocks, parts)], sem))
        total[...] = sum(parts[j].astype(f32) for j in range(half)).astype(bf16)
        wait(fetch([(total.at[pl.ds(0, rank)], shrink), (total.at[pl.ds(rank, rank)], expand)], sem, 1))

    return call(
        kernel,
        (1,),
        0,
        [HBM],
        [HBM] * 2,
        [array(rank, width)] * 2,
        [vmem(*blocks.shape), vmem(2 * rank, width), sems(3)],
        mib=16,
    )(*far(blocks))


def forward(spot, table, at, n, W, blocks, terms, back):
    rows, width = blocks[0][0].shape
    columns = W.shape[1]
    coarse = 2 if width % 512 == 0 else 1
    tile = width // coarse
    count = len(blocks)
    arrays = [b for block in blocks for b in block]

    def kernel(spot, *refs):
        flat, (W, term, back_term, other, back) = refs[: len(arrays)], refs[len(arrays) : len(arrays) + 5]
        out, rest, held, w, total, sides, sem, side_sem = refs[len(arrays) + 5 :]
        flat = iter(flat)
        mine = [[next(flat) for _ in block] for block in blocks]
        lefts = []
        for s, block in enumerate(mine):
            pick = [pltpu.make_async_copy(ref, held.at[s], side_sem.at[s]) for ref in block]
            if len(block) == 1:
                pick[0].start()
            else:
                one = look_up(spot, table, at + 2 * s + 1) == 1
                pl.when(one)(pick[0].start)
                pl.when(jnp.logical_not(one))(pick[1].start)
            lefts.append(pick[0])
        ins = Stream(W, w, [look_up(spot, table, at + 2 * s) for s in range(count)], width, sem)
        ins.start(6)
        own, theirs = pl.ds(0, rows), pl.ds(rows, rows)
        pairs = [term, other.at[own], back_term, other.at[theirs], back.at[back.shape[0] - 1]]
        for s in range(count):
            lefts[s].wait()
            for i in range(coarse):
                k = s * coarse + i
                ins.take(count * coarse)
                if k == count * coarse // 2:
                    added = fetch([(r, sides.at[i]) for i, r in enumerate(pairs)], side_sem, count)
                product = dot(held[s, :, pl.ds(i * tile, tile)], w[pl.ds(s * width + i * tile, tile)], 1, 0)
                if k == 0:
                    total[...] = product
                else:
                    total[...] += product
        wait(added)
        sides[0] = (total[...] + (sides[0].astype(f32) + sides[1].astype(f32))).astype(bf16)
        outs = fetch([(sides.at[0], out)], side_sem, count + 5)
        sides[2] = (sides[2].astype(f32) + sides[3].astype(f32) + sides[4].astype(f32)).astype(bf16)
        wait(outs + fetch([(sides.at[2], rest)], side_sem, count + 6))

    return call(
        kernel,
        (1,),
        1,
        [HBM] * (len(arrays) + 5),
        [HBM] * 2,
        [array(rows, columns), array(rows, width)],
        [
            vmem(count, rows, width),
            vmem(count * width, columns),
            pltpu.VMEM((rows, columns), f32),
            vmem(5, rows, columns),
            sems(4 * count),
            sems(count + 7),
        ],
    )(spot, *far(*arrays, W, *terms, back))


def chosen_of(spot, slots, ids, rank, half):
    ids = jnp.concatenate([r[...] for r in ids], axis=1)
    slot = jnp.zeros(ids.shape, jnp.int32)
    for a in range(slots.shape[0]):
        slot = jnp.where(ids == a, slots[a], slot)
    column = lax.broadcasted_iota(jnp.int32, (half * rank, ids.shape[1]), 0) // rank
    return jnp.where(slot == 2 * column + lax.rem(spot[0], 2), 1.0, 0.0).T > 0.5


def pieces(gathered, downs, ups, rank):
    half = gathered.shape[0]
    return [(gathered.at[j, pl.ds(0, rank)], downs.at[pl.ds(j * rank, rank)]) for j in range(half)] + [
        (gathered.at[j, pl.ds(rank, rank)], ups.at[pl.ds(j * rank, rank)]) for j in range(half)
    ]


def rows_of(X, dY, x, y, rows):
    top, bottom = pl.ds(0, rows), pl.ds(rows, rows)
    return [(X[0], x.at[top]), (X[1], x.at[bottom]), (dY[0], y.at[top]), (dY[1], y.at[bottom])]


def ids_spec(rows):
    return pl.BlockSpec((1, rows), lambda i, *_: (0, 0))


def low_parts(spot, slots, ids, Xs, dYs, gathered, rank, n):
    rows, width = Xs[0].shape
    half = gathered.shape[0]

    def kernel(spot, slots, id0, id1, X, X_other, dY, dY_other, gathered, out, x, y, downs, ups, part, sem):
        rights = pieces(gathered, downs, ups, rank)
        lefts = rows_of((X, X_other), (dY, dY_other), x, y, rows)
        ready = fetch(lefts[:2] + rights[:half], sem)
        more = fetch(lefts[2:] + rights[half:], sem, 2 + half)
        chosen = chosen_of(spot, slots, (id0, id1), rank, half)

        def pick(a, b):
            both = jnp.where(chosen, dot(a[...], b[...], 1, 1), 0)
            return sum(both[:, j * rank : (j + 1) * rank] for j in range(half))

        wait(ready)
        low = pick(x, downs)
        wait(more)
        part[...] = jnp.concatenate([low, pick(y, ups)], axis=1).astype(bf16)
        wait(fetch([(part, out.at[k]) for k in range(n)], sem, 4 + 2 * half))

    return call(
        kernel,
        (1,),
        2,
        [ids_spec(rows)] * 2 + [HBM] * 5,
        HBM,
        array(n, 2 * rows, 2 * rank),
        [vmem(2 * rows, width)] * 2
        + [vmem(half * rank, width)] * 2
        + [vmem(2 * rows, 2 * rank), sems(4 + 2 * half + n)],
    )(spot, slots, *ids, *far(*Xs, *dYs, gathered))


def adapters(spot, slots, ids, parts, Xs, dYs, gathered, rank):
    rows, width = Xs[0].shape
    half = gathered.shape[0]

    def kernel(spot, slots, id0, id1, parts, X, X_other, dY, dY_other, gathered, out, term, back, other, *scratch):
        x, y, downs, ups, grads, terms, sem, out_sem = scratch
        ins = fetch(
            rows_of((X, X_other), (dY, dY_other), x, y, rows) + pieces(gathered, downs, ups, rank), sem
        )
        chosen = chosen_of(spot, slots, (id0, id1), rank, half)
        total = sum(parts[k].astype(f32) for k in range(parts.shape[0]))
        low, grad = total[:, :rank].astype(bf16), (adapter_scale * total[:, rank:]).astype(bf16)
        zero = jnp.zeros((), bf16)
        low, grad = [jnp.where(chosen, jnp.concatenate([v] * half, axis=1), zero) for v in (low, grad)]
        wait(ins[:2])
        shrink = dot(grad, x[...], 0, 0).astype(bf16)
        for j in range(half):
            grads[j, :rank] = shrink[j * rank : (j + 1) * rank]
        wait(ins[2:4])
        expand = (adapter_scale * dot(low, y[...], 0, 0)).astype(bf16)
        for j in range(half):
            grads[j, rank:] = expand[j * rank : (j + 1) * rank]
        outs = fetch([(grads, out)], out_sem)
        wait(ins[4:])
        top, bottom = pl.ds(0, rows), pl.ds(rows, rows)
        terms[0] = (adapter_scale * dot(low, ups[...], 1, 0)).astype(bf16)
        outs += fetch([(terms.at[0, top], term), (terms.at[0, bottom], other.at[top])], out_sem, 1)
        terms[1] = dot(grad, downs[...], 1, 0).astype(bf16)
        outs += fetch([(terms.at[1, top], back), (terms.at[1, bottom], other.at[bottom])], out_sem, 3)
        wait(outs)

    return call(
        kernel,
        (1,),
        2,
        [ids_spec(rows)] * 2 + [pl.BlockSpec(memory_space=pltpu.VMEM)] + [HBM] * 5,
        [HBM] * 4,
        [array(half, 2 * rank, width), array(rows, width), array(rows, width), array(2 * rows, width)],
        [vmem(2 * rows, width)] * 2
        + [vmem(half * rank, width)] * 2
        + [vmem(half, 2 * rank, width), vmem(2, 2 * rows, width), sems(4 + 2 * half), sems(5)],
        mib=60,
        cost=GRADS,
    )(spot, slots, *ids, pltpu.with_memory_space_constraint(parts, pltpu.VMEM), *far(*Xs, *dYs, gathered))


def body(X, dY, W, A, B, adapter_rows, adapter_slot):
    rows, width = X.shape
    rank = A.shape[2]
    n, D = lax.axis_size("tensor"), lax.axis_size("dp")
    z, me = lax.axis_index("tensor"), lax.axis_index("dp")
    half = D // 2
    chips = [list(range(k, D, 2)) for k in (0, 1)]

    odd = me & 1
    up = [(d * n + i, d * n + i + 1) for d in range(D) for i in range(n - 1)]
    pairs = [[(a, b) if (a // n) % 2 == k else (b, a) for a, b in up] for k in (0, 1)]

    def along(x, k):
        return lax.ppermute(x, ("dp", "tensor"), pairs[k])

    table = []
    for i in range(n):
        for k in (0, 1):
            order = sorted(range(n), key=lambda d: (-abs(d - i), d))
            row = [k] + order
            for s in range(1, n):
                for way in (0, 1):
                    p = i if k == way else n - 1 - i
                    target = min(max(n - s + p, 0), n - 1)
                    row += [order.index(target if k == way else n - 1 - target), int(p < s)]
            p = i if k == 0 else n - 1 - i
            for s in range(n):
                source = (p - s) % n
                row += [source if k == 0 else n - 1 - source, int(p >= s)]
            table.append(row)
    steps_at, forward_at = 1 + n, 1 + n + 4 * (n - 1)
    spot = jnp.stack([2 * z + odd])

    arrived = [[X], [X]]
    arrived[0].append(along(X, 0))

    X_other, dY_other, rows_other = (exchange(v, "dp", 1) for v in (X, dY, adapter_rows))
    others = (X_other, dY_other, rows_other)
    own = own_adapter(A[0].T, after(B, *others)[0], half)
    gathered = swap(own, "dp", chips)
    arrived[1].append(along(after(X, own), 1))

    first, second, third = list(range(1, n - 1)), [n - 1], [n]
    backs = [backward(spot, table, first, after(dY, own, *others), W, n)]

    def onward(s, k, last):
        cost = LATE if s == n - 1 else SOON if (s, k) == (1, 1) else 10**3
        payload = add_on(spot, table, steps_at + 4 * (s - 1) + 2 * k, after(arrived[k][s], last), backs, cost)
        arrived[k].append(along(payload, k))
        return payload

    last = onward(1, 0, backs[0])
    last = onward(1, 1, last)

    ids = adapter_rows.reshape(1, rows), rows_other.reshape(1, rows)
    Xs, dYs = (X, X_other), (dY, dY_other)
    backs.append(backward(spot, table, second, after(dY, last), W, n))
    gathered = after(gathered, backs[1])
    part = low_parts(spot, adapter_slot, ids, Xs, dYs, gathered, rank, n)
    parts = swap(part, "tensor", None)

    last = part
    for s in range(2, n):
        last = onward(s, 0, last)
        if s == 2:
            own_back = backward(spot, table, third, after(dY, last), W, n)
            last = own_back
        last = onward(s, 1, last)
        if s == 2:
            parts = after(parts, last)
            mine, term, back_term, send = adapters(spot, adapter_slot, ids, parts, Xs, dYs, gathered, rank)
            arriving = swap(mine, "dp", chips)
            other = exchange(send, "dp", 1)
            last = send

    blocks = [(after(X, last),)] + [(arrived[0][s], arrived[1][n - s]) for s in range(1, n)]
    projected, rest = forward(spot, table, forward_at, n, W, blocks, (term, back_term, other), own_back)
    shrink, expand = add_up(after(arriving, projected), rank)
    activation = finish((arrived[0][n], arrived[1][n]), after(rest, shrink))
    return projected, activation, shrink.T[None], expand[None]


def solution(mesh):
    return jax.shard_map(
        body,
        mesh=mesh,
        in_specs=(
            P("dp", "tensor"),
            P("dp", "tensor"),
            P(None, "tensor"),
            P("dp", "tensor", None),
            P("dp", None, "tensor"),
            P("dp", None),
            P(),
        ),
        out_specs=(
            P("dp", "tensor"),
            P("dp", "tensor"),
            P("dp", "tensor", None),
            P("dp", None, "tensor"),
        ),
        check_vma=False,
    )
```

```python
import jax
import jax.numpy as jnp
from jax import lax
from jax.experimental import pallas as pl
from jax.experimental.pallas import tpu as pltpu
from jax.sharding import PartitionSpec as P

adapter_scale = 2.0
f32, bf16 = jnp.float32, jnp.bfloat16
HBM = pl.BlockSpec(memory_space=pltpu.HBM)
LATE = 10**12
GRADS = 10**10
BIG = 63
SOON = 10**10


def dot(a, b, ca, cb):
    return lax.dot_general(a, b, (((ca,), (cb,)), ((), ())), preferred_element_type=f32)


def exchange(x, axis, offset):
    size = lax.axis_size(axis)
    return lax.ppermute(x, axis, [(i, i ^ offset) for i in range(size)])


def swap(x, axis, groups):
    return lax.all_to_all(x, axis, 0, 0, axis_index_groups=groups, tiled=True)


def after(x, *earlier):
    return lax.optimization_barrier((x,) + earlier)[0]


def call(kernel, grid, prefetch, ins, outs, shapes, scratch, mib=BIG, cost=10**3):
    return pl.pallas_call(
        kernel,
        grid_spec=pltpu.PrefetchScalarGridSpec(
            num_scalar_prefetch=prefetch, grid=grid, in_specs=ins, out_specs=outs, scratch_shapes=list(scratch)
        ),
        out_shape=shapes,
        cost_estimate=pl.CostEstimate(flops=cost, bytes_accessed=1, transcendentals=0),
        compiler_params=pltpu.CompilerParams(vmem_limit_bytes=mib * 2**20),
    )


def array(*shape):
    return pltpu.HBM(shape, bf16)


def far(*xs):
    return [pltpu.with_memory_space_constraint(x, pltpu.HBM) for x in xs]


def vmem(*shape):
    return pltpu.VMEM(shape, bf16)


def look_up(spot, table, column):
    value = jnp.int32(table[0][column])
    for i, row in enumerate(table[1:], 1):
        value = jnp.where(spot[0] == i, row[column], value)
    return value


def sems(count):
    return pltpu.SemaphoreType.DMA((count,))


def fetch(copies, sem, first=0):
    copies = [pltpu.make_async_copy(a, b, sem.at[first + i]) for i, (a, b) in enumerate(copies)]
    for c in copies:
        c.start()
    return copies


def wait(copies):
    for c in copies:
        c.wait()


def own_adapter(A, B, half):
    rank, width = B.shape

    def kernel(A, B, out, both, sem):
        wait(fetch([(A, both.at[pl.ds(0, rank)]), (B, both.at[pl.ds(rank, rank)])], sem))
        wait(fetch([(both, out.at[j]) for j in range(half)], sem, 2))

    return call(
        kernel, (1,), 0, [HBM, HBM], HBM, array(half, 2 * rank, width), [vmem(2 * rank, width), sems(2 + half)], mib=4
    )(*far(A, B))


class Stream:
    def __init__(self, W, w, starts, size, sem):
        chunk = size // 4 if size % 512 == 0 else size
        self.copies, self.started, self.done = [], 0, 0
        for b, start in enumerate(starts):
            for i in range(size // chunk):
                source = W.at[pl.ds(pl.multiple_of(start * size + i * chunk, chunk), chunk)]
                k = len(self.copies)
                self.copies.append(pltpu.make_async_copy(source, w.at[pl.ds(b * size + i * chunk, chunk)], sem.at[k]))

    def start(self, count):
        for c in self.copies[self.started : self.started + count]:
            c.start()
        self.started += count

    def take(self, parts):
        for _ in range(len(self.copies) // parts):
            self.copies[self.done].wait()
            self.done += 1
            self.start(1)


def backward_blocks(y, w, done, out, stream, size, coarse, sem):
    blocks = done.shape[0]
    tile = size // coarse
    outs = []
    for b in range(blocks):
        for i in range(coarse):
            stream.take(blocks * coarse)
            span = pl.ds(i * tile, tile)
            done[b, :, span] = dot(y, w[pl.ds(b * size + i * tile, tile)], 1, 1).astype(bf16)
            outs += fetch([(done.at[b, :, span], out.at[b, :, span])], sem, b * coarse + i)
    return outs


def backward(spot, table, columns, dY, W, n):
    rows, width = dY.shape
    size = W.shape[0] // n
    blocks = len(columns)
    coarse = 1 if size % 512 else 2 if blocks > 1 else 4

    def kernel(spot, dY, W, out, y, w, done, sem, out_sem, y_sem):
        ready = fetch([(dY, y)], y_sem)
        ins = Stream(W, w, [look_up(spot, table, c) for c in columns], size, sem)
        ins.start(4 if blocks > 1 else 2)
        wait(ready)
        wait(backward_blocks(y[...], w, done, out, ins, size, coarse, out_sem))

    return call(
        kernel,
        (1,),
        1,
        [HBM, HBM],
        HBM,
        array(blocks, rows, size),
        [vmem(rows, width), vmem(blocks * size, width), vmem(blocks, rows, size), sems(4 * blocks), sems(4 * blocks), sems(1)],
    )(spot, *far(dY, W))


def add_on(spot, table, at, arrived, backs, cost):
    rows, width = arrived.shape
    steps = 4
    size = rows // steps
    count = backs[0].shape[0]

    def kernel(spot, arrived, *refs):
        backs, (out, a, b, sem) = refs[:-4], refs[-4:]
        parts = [pl.ds(i * size, size) for i in range(steps)]
        add, block = look_up(spot, table, at + 1) == 1, look_up(spot, table, at)
        ins = [pltpu.make_async_copy(arrived.at[p], a.at[p], sem.at[i]) for i, p in enumerate(parts)]
        adds = [
            [pltpu.make_async_copy(r.at[lax.rem(block, count), p], b.at[p], sem.at[steps + i]) for r in backs]
            for i, p in enumerate(parts)
        ]
        outs = [pltpu.make_async_copy(a.at[p], out.at[p], sem.at[2 * steps + i]) for i, p in enumerate(parts)]
        for i in range(steps):
            ins[i].start()
            for k in range(len(backs)):
                pl.when(add & (lax.div(block, count) == k))(adds[i][k].start)
        for i, p in enumerate(parts):
            ins[i].wait()

            @pl.when(add)
            def _():
                adds[i][0].wait()
                a[p] = (a[p].astype(f32) + b[p].astype(f32)).astype(bf16)

            outs[i].start()
        wait(outs)

    return call(
        kernel,
        (1,),
        1,
        [HBM] * (1 + len(backs)),
        HBM,
        array(rows, width),
        [vmem(rows, width), vmem(rows, width), sems(3 * steps)],
        mib=8,
        cost=cost,
    )(spot, *far(arrived, *backs))


def finish(arrived, rest):
    rows, width = rest.shape
    steps = 4
    size = rows // steps

    def kernel(one, two, rest, out, held, done, sem):
        refs = [one, two, rest]
        spans = [pl.ds(i * size, size) for i in range(steps)]
        ins = [
            fetch([(r.at[p], held.at[k, p]) for k, r in enumerate(refs)], sem, i * len(refs))
            for i, p in enumerate(spans)
        ]
        outs = []
        for i, p in enumerate(spans):
            wait(ins[i])
            done[p] = (held[0, p].astype(f32) + held[1, p].astype(f32) + held[2, p].astype(f32)).astype(bf16)
            outs += fetch([(done.at[p], out.at[p])], sem, steps * len(refs) + i)
        wait(outs)

    return call(
        kernel,
        (1,),
        0,
        [HBM] * 3,
        HBM,
        array(rows, width),
        [vmem(3, rows, width), vmem(rows, width), sems(4 * steps)],
        mib=16,
    )(*far(*arrived, rest))


def add_up(blocks, rank):
    half, _, width = blocks.shape

    def kernel(blocks, shrink, expand, parts, total, sem):
        wait(fetch([(blocks, parts)], sem))
        total[...] = sum(parts[j].astype(f32) for j in range(half)).astype(bf16)
        wait(fetch([(total.at[pl.ds(0, rank)], shrink), (total.at[pl.ds(rank, rank)], expand)], sem, 1))

    return call(
        kernel,
        (1,),
        0,
        [HBM],
        [HBM] * 2,
        [array(rank, width)] * 2,
        [vmem(*blocks.shape), vmem(2 * rank, width), sems(3)],
        mib=16,
    )(*far(blocks))


def forward(spot, table, at, n, W, blocks, terms, back):
    rows, width = blocks[0][0].shape
    columns = W.shape[1]
    coarse = 2 if width % 512 == 0 else 1
    tile = width // coarse
    count = len(blocks)
    arrays = [b for block in blocks for b in block]

    def kernel(spot, *refs):
        flat, (W, term, back_term, other, back) = refs[: len(arrays)], refs[len(arrays) : len(arrays) + 5]
        out, rest, held, w, total, sides, sem, side_sem = refs[len(arrays) + 5 :]
        flat = iter(flat)
        mine = [[next(flat) for _ in block] for block in blocks]
        lefts = []
        for s, block in enumerate(mine):
            pick = [pltpu.make_async_copy(ref, held.at[s], side_sem.at[s]) for ref in block]
            if len(block) == 1:
                pick[0].start()
            else:
                one = look_up(spot, table, at + 2 * s + 1) == 1
                pl.when(one)(pick[0].start)
                pl.when(jnp.logical_not(one))(pick[1].start)
            lefts.append(pick[0])
        ins = Stream(W, w, [look_up(spot, table, at + 2 * s) for s in range(count)], width, sem)
        ins.start(6)
        own, theirs = pl.ds(0, rows), pl.ds(rows, rows)
        pairs = [term, other.at[own], back_term, other.at[theirs], back.at[back.shape[0] - 1]]
        for s in range(count):
            lefts[s].wait()
            for i in range(coarse):
                k = s * coarse + i
                ins.take(count * coarse)
                if k == count * coarse // 2:
                    added = fetch([(r, sides.at[i]) for i, r in enumerate(pairs)], side_sem, count)
                product = dot(held[s, :, pl.ds(i * tile, tile)], w[pl.ds(s * width + i * tile, tile)], 1, 0)
                if k == 0:
                    total[...] = product
                else:
                    total[...] += product
        wait(added)
        sides[0] = (total[...] + (sides[0].astype(f32) + sides[1].astype(f32))).astype(bf16)
        outs = fetch([(sides.at[0], out)], side_sem, count + 5)
        sides[2] = (sides[2].astype(f32) + sides[3].astype(f32) + sides[4].astype(f32)).astype(bf16)
        wait(outs + fetch([(sides.at[2], rest)], side_sem, count + 6))

    return call(
        kernel,
        (1,),
        1,
        [HBM] * (len(arrays) + 5),
        [HBM] * 2,
        [array(rows, columns), array(rows, width)],
        [
            vmem(count, rows, width),
            vmem(count * width, columns),
            pltpu.VMEM((rows, columns), f32),
            vmem(5, rows, columns),
            sems(4 * count),
            sems(count + 7),
        ],
    )(spot, *far(*arrays, W, *terms, back))


def chosen_of(spot, slots, ids, rank, half):
    ids = jnp.concatenate([r[...] for r in ids], axis=1)
    slot = jnp.zeros(ids.shape, jnp.int32)
    for a in range(slots.shape[0]):
        slot = jnp.where(ids == a, slots[a], slot)
    column = lax.broadcasted_iota(jnp.int32, (half * rank, ids.shape[1]), 0) // rank
    return jnp.where(slot == 2 * column + lax.rem(spot[0], 2), 1.0, 0.0).T > 0.5


def pieces(gathered, downs, ups, rank):
    half = gathered.shape[0]
    return [(gathered.at[j, pl.ds(0, rank)], downs.at[pl.ds(j * rank, rank)]) for j in range(half)] + [
        (gathered.at[j, pl.ds(rank, rank)], ups.at[pl.ds(j * rank, rank)]) for j in range(half)
    ]


def rows_of(X, dY, x, y, rows):
    top, bottom = pl.ds(0, rows), pl.ds(rows, rows)
    return [(X[0], x.at[top]), (X[1], x.at[bottom]), (dY[0], y.at[top]), (dY[1], y.at[bottom])]


def ids_spec(rows):
    return pl.BlockSpec((1, rows), lambda i, *_: (0, 0))


def low_parts(spot, slots, ids, Xs, dYs, gathered, rank, n):
    rows, width = Xs[0].shape
    half = gathered.shape[0]

    def kernel(spot, slots, id0, id1, X, X_other, dY, dY_other, gathered, out, x, y, downs, ups, part, sem):
        rights = pieces(gathered, downs, ups, rank)
        lefts = rows_of((X, X_other), (dY, dY_other), x, y, rows)
        ready = fetch(lefts[:2] + rights[:half], sem)
        more = fetch(lefts[2:] + rights[half:], sem, 2 + half)
        chosen = chosen_of(spot, slots, (id0, id1), rank, half)

        def pick(a, b):
            both = jnp.where(chosen, dot(a[...], b[...], 1, 1), 0)
            return sum(both[:, j * rank : (j + 1) * rank] for j in range(half))

        wait(ready)
        low = pick(x, downs)
        wait(more)
        part[...] = jnp.concatenate([low, pick(y, ups)], axis=1).astype(bf16)
        wait(fetch([(part, out)], sem, 4 + 2 * half))

    return call(
        kernel,
        (1,),
        2,
        [ids_spec(rows)] * 2 + [HBM] * 5,
        HBM,
        array(2 * rows, 2 * rank),
        [vmem(2 * rows, width)] * 2
        + [vmem(half * rank, width)] * 2
        + [vmem(2 * rows, 2 * rank), sems(4 + 2 * half + n)],
    )(spot, slots, *ids, *far(*Xs, *dYs, gathered))


def adapters(spot, slots, ids, few, Xs, dYs, gathered, rank):
    rows, width = Xs[0].shape
    half = gathered.shape[0]

    def kernel(spot, slots, id0, id1, *refs):
        parts, (X, X_other, dY, dY_other, gathered, out, term, back, other, *scratch) = refs[: len(few)], refs[len(few) :]
        x, y, downs, ups, grads, terms, sem, out_sem = scratch
        ins = fetch(
            rows_of((X, X_other), (dY, dY_other), x, y, rows) + pieces(gathered, downs, ups, rank), sem
        )
        chosen = chosen_of(spot, slots, (id0, id1), rank, half)
        total = sum(p[...].astype(f32) for p in parts)
        low, grad = total[:, :rank].astype(bf16), (adapter_scale * total[:, rank:]).astype(bf16)
        zero = jnp.zeros((), bf16)
        low, grad = [jnp.where(chosen, jnp.concatenate([v] * half, axis=1), zero) for v in (low, grad)]
        wait(ins[:2])
        shrink = dot(grad, x[...], 0, 0).astype(bf16)
        for j in range(half):
            grads[j, :rank] = shrink[j * rank : (j + 1) * rank]
        wait(ins[2:4])
        expand = (adapter_scale * dot(low, y[...], 0, 0)).astype(bf16)
        for j in range(half):
            grads[j, rank:] = expand[j * rank : (j + 1) * rank]
        outs = fetch([(grads, out)], out_sem)
        wait(ins[4:])
        top, bottom = pl.ds(0, rows), pl.ds(rows, rows)
        terms[0] = (adapter_scale * dot(low, ups[...], 1, 0)).astype(bf16)
        outs += fetch([(terms.at[0, top], term), (terms.at[0, bottom], other.at[top])], out_sem, 1)
        terms[1] = dot(grad, downs[...], 1, 0).astype(bf16)
        outs += fetch([(terms.at[1, top], back), (terms.at[1, bottom], other.at[bottom])], out_sem, 3)
        wait(outs)

    return call(
        kernel,
        (1,),
        2,
        [ids_spec(rows)] * 2 + [pl.BlockSpec(memory_space=pltpu.VMEM)] * len(few) + [HBM] * 5,
        [HBM] * 4,
        [array(half, 2 * rank, width), array(rows, width), array(rows, width), array(2 * rows, width)],
        [vmem(2 * rows, width)] * 2
        + [vmem(half * rank, width)] * 2
        + [vmem(half, 2 * rank, width), vmem(2, 2 * rows, width), sems(4 + 2 * half), sems(5)],
        mib=60,
        cost=GRADS,
    )(spot, slots, *ids, *[pltpu.with_memory_space_constraint(p, pltpu.VMEM) for p in few], *far(*Xs, *dYs, gathered))


def body(X, dY, W, A, B, adapter_rows, adapter_slot):
    rows, width = X.shape
    rank = A.shape[2]
    n, D = lax.axis_size("tensor"), lax.axis_size("dp")
    z, me = lax.axis_index("tensor"), lax.axis_index("dp")
    half = D // 2
    chips = [list(range(k, D, 2)) for k in (0, 1)]

    odd = me & 1
    up = [(d * n + i, d * n + i + 1) for d in range(D) for i in range(n - 1)]
    pairs = [[(a, b) if (a // n) % 2 == k else (b, a) for a, b in up] for k in (0, 1)]

    def along(x, k):
        return lax.ppermute(x, ("dp", "tensor"), pairs[k])

    table = []
    for i in range(n):
        for k in (0, 1):
            order = sorted(range(n), key=lambda d: (-abs(d - i), d))
            row = [k] + order
            for s in range(1, n):
                for way in (0, 1):
                    p = i if k == way else n - 1 - i
                    target = min(max(n - s + p, 0), n - 1)
                    row += [order.index(target if k == way else n - 1 - target), int(p < s)]
            p = i if k == 0 else n - 1 - i
            for s in range(n):
                source = (p - s) % n
                row += [source if k == 0 else n - 1 - source, int(p >= s)]
            table.append(row)
    steps_at, forward_at = 1 + n, 1 + n + 4 * (n - 1)
    spot = jnp.stack([2 * z + odd])

    arrived = [[X], [X]]
    arrived[0].append(along(X, 0))

    X_other, dY_other, rows_other = (exchange(v, "dp", 1) for v in (X, dY, adapter_rows))
    others = (X_other, dY_other, rows_other)
    own = own_adapter(A[0].T, after(B, *others)[0], half)
    gathered = swap(own, "dp", chips)
    arrived[1].append(along(after(X, own), 1))

    first, second, third = list(range(1, n - 1)), [n - 1], [n]
    backs = [backward(spot, table, first, after(dY, own, *others), W, n)]

    def onward(s, k, last):
        cost = LATE if s == n - 1 else SOON if (s, k) == (1, 1) else 10**3
        payload = add_on(spot, table, steps_at + 4 * (s - 1) + 2 * k, after(arrived[k][s], last), backs, cost)
        arrived[k].append(along(payload, k))
        return payload

    last = onward(1, 0, backs[0])
    last = onward(1, 1, last)

    ids = adapter_rows.reshape(1, rows), rows_other.reshape(1, rows)
    Xs, dYs = (X, X_other), (dY, dY_other)
    backs.append(backward(spot, table, second, after(dY, last), W, n))
    gathered = after(gathered, backs[1])
    part = low_parts(spot, adapter_slot, ids, Xs, dYs, gathered, rank, n)
    parts = [part] + [exchange(part, "tensor", k) for k in range(1, n)]

    last = part
    for s in range(2, n):
        last = onward(s, 0, last)
        if s == 2:
            own_back = backward(spot, table, third, after(dY, last), W, n)
            last = own_back
        last = onward(s, 1, last)
        if s == 2:
            parts = [after(p, last) for p in parts]
            mine, term, back_term, send = adapters(spot, adapter_slot, ids, parts, Xs, dYs, gathered, rank)
            arriving = swap(mine, "dp", chips)
            other = exchange(send, "dp", 1)
            last = send

    blocks = [(after(X, last),)] + [(arrived[0][s], arrived[1][n - s]) for s in range(1, n)]
    projected, rest = forward(spot, table, forward_at, n, W, blocks, (term, back_term, other), own_back)
    shrink, expand = add_up(after(arriving, projected), rank)
    activation = finish((arrived[0][n], arrived[1][n]), after(rest, shrink))
    return projected, activation, shrink.T[None], expand[None]


def solution(mesh):
    return jax.shard_map(
        body,
        mesh=mesh,
        in_specs=(
            P("dp", "tensor"),
            P("dp", "tensor"),
            P(None, "tensor"),
            P("dp", "tensor", None),
            P("dp", None, "tensor"),
            P("dp", None),
            P(),
        ),
        out_specs=(
            P("dp", "tensor"),
            P("dp", "tensor"),
            P("dp", "tensor", None),
            P("dp", None, "tensor"),
        ),
        check_vma=False,
    )
```

```python
import jax
import jax.numpy as jnp
from jax import lax
from jax.experimental import pallas as pl
from jax.experimental.pallas import tpu as pltpu
from jax.sharding import PartitionSpec as P

adapter_scale = 2.0
f32, bf16 = jnp.float32, jnp.bfloat16
HBM = pl.BlockSpec(memory_space=pltpu.HBM)
LATE = 10**12
GRADS = 10**10
BIG = 63
SOON = 10**10


def dot(a, b, ca, cb):
    return lax.dot_general(a, b, (((ca,), (cb,)), ((), ())), preferred_element_type=f32)


def exchange(x, axis, offset):
    size = lax.axis_size(axis)
    return lax.ppermute(x, axis, [(i, i ^ offset) for i in range(size)])


def swap(x, axis, groups):
    return lax.all_to_all(x, axis, 0, 0, axis_index_groups=groups, tiled=True)


def after(x, *earlier):
    return lax.optimization_barrier((x,) + earlier)[0]


def call(kernel, grid, prefetch, ins, outs, shapes, scratch, mib=BIG, cost=10**3):
    return pl.pallas_call(
        kernel,
        grid_spec=pltpu.PrefetchScalarGridSpec(
            num_scalar_prefetch=prefetch, grid=grid, in_specs=ins, out_specs=outs, scratch_shapes=list(scratch)
        ),
        out_shape=shapes,
        cost_estimate=pl.CostEstimate(flops=cost, bytes_accessed=1, transcendentals=0),
        compiler_params=pltpu.CompilerParams(vmem_limit_bytes=mib * 2**20),
    )


def array(*shape):
    return pltpu.HBM(shape, bf16)


def far(*xs):
    return [pltpu.with_memory_space_constraint(x, pltpu.HBM) for x in xs]


def vmem(*shape):
    return pltpu.VMEM(shape, bf16)


def look_up(spot, table, column):
    value = jnp.int32(table[0][column])
    for i, row in enumerate(table[1:], 1):
        value = jnp.where(spot[0] == i, row[column], value)
    return value


def sems(count):
    return pltpu.SemaphoreType.DMA((count,))


def fetch(copies, sem, first=0):
    copies = [pltpu.make_async_copy(a, b, sem.at[first + i]) for i, (a, b) in enumerate(copies)]
    for c in copies:
        c.start()
    return copies


def wait(copies):
    for c in copies:
        c.wait()


def own_adapter(A, B, half):
    rank, width = B.shape

    def kernel(A, B, out, both, sem):
        wait(fetch([(A, both.at[pl.ds(0, rank)]), (B, both.at[pl.ds(rank, rank)])], sem))
        wait(fetch([(both, out.at[j]) for j in range(half)], sem, 2))

    return call(
        kernel, (1,), 0, [HBM, HBM], HBM, array(half, 2 * rank, width), [vmem(2 * rank, width), sems(2 + half)], mib=4
    )(*far(A, B))


class Stream:
    def __init__(self, W, w, starts, size, sem):
        chunk = size // 4 if size % 512 == 0 else size
        self.copies, self.started, self.done = [], 0, 0
        for b, start in enumerate(starts):
            for i in range(size // chunk):
                source = W.at[pl.ds(pl.multiple_of(start * size + i * chunk, chunk), chunk)]
                k = len(self.copies)
                self.copies.append(pltpu.make_async_copy(source, w.at[pl.ds(b * size + i * chunk, chunk)], sem.at[k]))

    def start(self, count):
        for c in self.copies[self.started : self.started + count]:
            c.start()
        self.started += count

    def take(self, parts):
        for _ in range(len(self.copies) // parts):
            self.copies[self.done].wait()
            self.done += 1
            self.start(1)


def backward_blocks(y, w, done, out, stream, size, coarse, sem):
    blocks = done.shape[0]
    tile = size // coarse
    outs = []
    for b in range(blocks):
        for i in range(coarse):
            stream.take(blocks * coarse)
            span = pl.ds(i * tile, tile)
            done[b, :, span] = dot(y, w[pl.ds(b * size + i * tile, tile)], 1, 1).astype(bf16)
            outs += fetch([(done.at[b, :, span], out.at[b, :, span])], sem, b * coarse + i)
    return outs


def backward(spot, table, columns, dY, W, n):
    rows, width = dY.shape
    size = W.shape[0] // n
    blocks = len(columns)
    coarse = 1 if size % 512 else 2 if blocks > 1 else 4

    def kernel(spot, dY, W, out, y, w, done, sem, out_sem, y_sem):
        ready = fetch([(dY, y)], y_sem)
        ins = Stream(W, w, [look_up(spot, table, c) for c in columns], size, sem)
        ins.start(4 if blocks > 1 else 2)
        wait(ready)
        wait(backward_blocks(y[...], w, done, out, ins, size, coarse, out_sem))

    return call(
        kernel,
        (1,),
        1,
        [HBM, HBM],
        HBM,
        array(blocks, rows, size),
        [vmem(rows, width), vmem(blocks * size, width), vmem(blocks, rows, size), sems(4 * blocks), sems(4 * blocks), sems(1)],
    )(spot, *far(dY, W))


def add_on(spot, table, at, arrived, backs, cost):
    rows, width = arrived.shape
    steps = 4
    size = rows // steps
    count = backs[0].shape[0]

    def kernel(spot, arrived, *refs):
        backs, (out, a, b, sem) = refs[:-4], refs[-4:]
        parts = [pl.ds(i * size, size) for i in range(steps)]
        add, block = look_up(spot, table, at + 1) == 1, look_up(spot, table, at)
        ins = [pltpu.make_async_copy(arrived.at[p], a.at[p], sem.at[i]) for i, p in enumerate(parts)]
        adds = [
            [pltpu.make_async_copy(r.at[lax.rem(block, count), p], b.at[p], sem.at[steps + i]) for r in backs]
            for i, p in enumerate(parts)
        ]
        outs = [pltpu.make_async_copy(a.at[p], out.at[p], sem.at[2 * steps + i]) for i, p in enumerate(parts)]
        for i in range(steps):
            ins[i].start()
            for k in range(len(backs)):
                pl.when(add & (lax.div(block, count) == k))(adds[i][k].start)
        for i, p in enumerate(parts):
            ins[i].wait()

            @pl.when(add)
            def _():
                adds[i][0].wait()
                a[p] = (a[p].astype(f32) + b[p].astype(f32)).astype(bf16)

            outs[i].start()
        wait(outs)

    return call(
        kernel,
        (1,),
        1,
        [HBM] * (1 + len(backs)),
        HBM,
        array(rows, width),
        [vmem(rows, width), vmem(rows, width), sems(3 * steps)],
        mib=8,
        cost=cost,
    )(spot, *far(arrived, *backs))


def finish(arrived, rest, blocks, rank):
    rows, width = rest.shape
    half = blocks.shape[0]
    steps = 4
    size = rows // steps

    def kernel(one, two, rest, blocks, out, shrink, expand, held, done, parts, total, sem, more):
        refs = [one, two, rest]
        spans = [pl.ds(i * size, size) for i in range(steps)]
        ins = [
            fetch([(r.at[p], held.at[k, p]) for k, r in enumerate(refs)], sem, i * len(refs))
            for i, p in enumerate(spans)
        ]
        gradients = fetch([(blocks, parts)], more)
        outs = []
        for i, p in enumerate(spans):
            wait(ins[i])
            done[p] = (held[0, p].astype(f32) + held[1, p].astype(f32) + held[2, p].astype(f32)).astype(bf16)
            outs += fetch([(done.at[p], out.at[p])], sem, steps * len(refs) + i)
        wait(gradients)
        total[...] = sum(parts[j].astype(f32) for j in range(half)).astype(bf16)
        outs += fetch([(total.at[pl.ds(0, rank)], shrink), (total.at[pl.ds(rank, rank)], expand)], more, 1)
        wait(outs)

    return call(
        kernel,
        (1,),
        0,
        [HBM] * 4,
        [HBM] * 3,
        [array(rows, width), array(rank, width), array(rank, width)],
        [vmem(3, rows, width), vmem(rows, width), vmem(*blocks.shape), vmem(2 * rank, width), sems(4 * steps), sems(3)],
        mib=16,
    )(*far(*arrived, rest, blocks))


def forward(spot, table, at, n, W, blocks, terms, back):
    rows, width = blocks[0][0].shape
    columns = W.shape[1]
    coarse = 2 if width % 512 == 0 else 1
    tile = width // coarse
    count = len(blocks)
    arrays = [b for block in blocks for b in block]

    def kernel(spot, *refs):
        flat, (W, term, back_term, other, back) = refs[: len(arrays)], refs[len(arrays) : len(arrays) + 5]
        out, rest, held, w, total, sides, sem, side_sem = refs[len(arrays) + 5 :]
        flat = iter(flat)
        mine = [[next(flat) for _ in block] for block in blocks]
        lefts = []
        for s, block in enumerate(mine):
            pick = [pltpu.make_async_copy(ref, held.at[s], side_sem.at[s]) for ref in block]
            if len(block) == 1:
                pick[0].start()
            else:
                one = look_up(spot, table, at + 2 * s + 1) == 1
                pl.when(one)(pick[0].start)
                pl.when(jnp.logical_not(one))(pick[1].start)
            lefts.append(pick[0])
        ins = Stream(W, w, [look_up(spot, table, at + 2 * s) for s in range(count)], width, sem)
        ins.start(6)
        own, theirs = pl.ds(0, rows), pl.ds(rows, rows)
        pairs = [term, other.at[own], back_term, other.at[theirs], back.at[back.shape[0] - 1]]
        for s in range(count):
            lefts[s].wait()
            for i in range(coarse):
                k = s * coarse + i
                ins.take(count * coarse)
                if k == count * coarse // 2:
                    added = fetch([(r, sides.at[i]) for i, r in enumerate(pairs)], side_sem, count)
                product = dot(held[s, :, pl.ds(i * tile, tile)], w[pl.ds(s * width + i * tile, tile)], 1, 0)
                if k == 0:
                    total[...] = product
                else:
                    total[...] += product
        wait(added)
        sides[0] = (total[...] + (sides[0].astype(f32) + sides[1].astype(f32))).astype(bf16)
        outs = fetch([(sides.at[0], out)], side_sem, count + 5)
        sides[2] = (sides[2].astype(f32) + sides[3].astype(f32) + sides[4].astype(f32)).astype(bf16)
        wait(outs + fetch([(sides.at[2], rest)], side_sem, count + 6))

    return call(
        kernel,
        (1,),
        1,
        [HBM] * (len(arrays) + 5),
        [HBM] * 2,
        [array(rows, columns), array(rows, width)],
        [
            vmem(count, rows, width),
            vmem(count * width, columns),
            pltpu.VMEM((rows, columns), f32),
            vmem(5, rows, columns),
            sems(4 * count),
            sems(count + 7),
        ],
    )(spot, *far(*arrays, W, *terms, back))


def chosen_of(spot, slots, ids, rank, half):
    ids = jnp.concatenate([r[...] for r in ids], axis=1)
    slot = jnp.zeros(ids.shape, jnp.int32)
    for a in range(slots.shape[0]):
        slot = jnp.where(ids == a, slots[a], slot)
    column = lax.broadcasted_iota(jnp.int32, (half * rank, ids.shape[1]), 0) // rank
    return jnp.where(slot == 2 * column + lax.rem(spot[0], 2), 1.0, 0.0).T > 0.5


def pieces(gathered, downs, ups, rank):
    half = gathered.shape[0]
    return [(gathered.at[j, pl.ds(0, rank)], downs.at[pl.ds(j * rank, rank)]) for j in range(half)] + [
        (gathered.at[j, pl.ds(rank, rank)], ups.at[pl.ds(j * rank, rank)]) for j in range(half)
    ]


def rows_of(X, dY, x, y, rows):
    top, bottom = pl.ds(0, rows), pl.ds(rows, rows)
    return [(X[0], x.at[top]), (X[1], x.at[bottom]), (dY[0], y.at[top]), (dY[1], y.at[bottom])]


def ids_spec(rows):
    return pl.BlockSpec((1, rows), lambda i, *_: (0, 0))


def low_parts(spot, slots, ids, Xs, dYs, gathered, rank, n):
    rows, width = Xs[0].shape
    half = gathered.shape[0]

    def kernel(spot, slots, id0, id1, X, X_other, dY, dY_other, gathered, out, x, y, downs, ups, part, sem):
        rights = pieces(gathered, downs, ups, rank)
        lefts = rows_of((X, X_other), (dY, dY_other), x, y, rows)
        ready = fetch(lefts[:2] + rights[:half], sem)
        more = fetch(lefts[2:] + rights[half:], sem, 2 + half)
        chosen = chosen_of(spot, slots, (id0, id1), rank, half)

        def pick(a, b):
            both = jnp.where(chosen, dot(a[...], b[...], 1, 1), 0)
            return sum(both[:, j * rank : (j + 1) * rank] for j in range(half))

        wait(ready)
        low = pick(x, downs)
        wait(more)
        part[...] = jnp.concatenate([low, pick(y, ups)], axis=1).astype(bf16)
        wait(fetch([(part, out)], sem, 4 + 2 * half))

    return call(
        kernel,
        (1,),
        2,
        [ids_spec(rows)] * 2 + [HBM] * 5,
        HBM,
        array(2 * rows, 2 * rank),
        [vmem(2 * rows, width)] * 2
        + [vmem(half * rank, width)] * 2
        + [vmem(2 * rows, 2 * rank), sems(4 + 2 * half + n)],
    )(spot, slots, *ids, *far(*Xs, *dYs, gathered))


def adapters(spot, slots, ids, few, Xs, dYs, gathered, rank):
    rows, width = Xs[0].shape
    half = gathered.shape[0]

    def kernel(spot, slots, id0, id1, *refs):
        parts, (X, X_other, dY, dY_other, gathered, out, term, back, other, *scratch) = refs[: len(few)], refs[len(few) :]
        x, y, downs, ups, grads, terms, sem, out_sem = scratch
        ins = fetch(
            rows_of((X, X_other), (dY, dY_other), x, y, rows) + pieces(gathered, downs, ups, rank), sem
        )
        chosen = chosen_of(spot, slots, (id0, id1), rank, half)
        total = sum(p[...].astype(f32) for p in parts)
        low, grad = total[:, :rank].astype(bf16), (adapter_scale * total[:, rank:]).astype(bf16)
        zero = jnp.zeros((), bf16)
        low, grad = [jnp.where(chosen, jnp.concatenate([v] * half, axis=1), zero) for v in (low, grad)]
        wait(ins[:2])
        shrink = dot(grad, x[...], 0, 0).astype(bf16)
        for j in range(half):
            grads[j, :rank] = shrink[j * rank : (j + 1) * rank]
        wait(ins[2:4])
        expand = (adapter_scale * dot(low, y[...], 0, 0)).astype(bf16)
        for j in range(half):
            grads[j, rank:] = expand[j * rank : (j + 1) * rank]
        outs = fetch([(grads, out)], out_sem)
        wait(ins[4:])
        top, bottom = pl.ds(0, rows), pl.ds(rows, rows)
        terms[0] = (adapter_scale * dot(low, ups[...], 1, 0)).astype(bf16)
        outs += fetch([(terms.at[0, top], term), (terms.at[0, bottom], other.at[top])], out_sem, 1)
        terms[1] = dot(grad, downs[...], 1, 0).astype(bf16)
        outs += fetch([(terms.at[1, top], back), (terms.at[1, bottom], other.at[bottom])], out_sem, 3)
        wait(outs)

    return call(
        kernel,
        (1,),
        2,
        [ids_spec(rows)] * 2 + [pl.BlockSpec(memory_space=pltpu.VMEM)] * len(few) + [HBM] * 5,
        [HBM] * 4,
        [array(half, 2 * rank, width), array(rows, width), array(rows, width), array(2 * rows, width)],
        [vmem(2 * rows, width)] * 2
        + [vmem(half * rank, width)] * 2
        + [vmem(half, 2 * rank, width), vmem(2, 2 * rows, width), sems(4 + 2 * half), sems(5)],
        mib=60,
        cost=GRADS,
    )(spot, slots, *ids, *[pltpu.with_memory_space_constraint(p, pltpu.VMEM) for p in few], *far(*Xs, *dYs, gathered))


def body(X, dY, W, A, B, adapter_rows, adapter_slot):
    rows, width = X.shape
    rank = A.shape[2]
    n, D = lax.axis_size("tensor"), lax.axis_size("dp")
    z, me = lax.axis_index("tensor"), lax.axis_index("dp")
    half = D // 2
    chips = [list(range(k, D, 2)) for k in (0, 1)]

    odd = me & 1
    up = [(d * n + i, d * n + i + 1) for d in range(D) for i in range(n - 1)]
    pairs = [[(a, b) if (a // n) % 2 == k else (b, a) for a, b in up] for k in (0, 1)]

    def along(x, k):
        return lax.ppermute(x, ("dp", "tensor"), pairs[k])

    table = []
    for i in range(n):
        for k in (0, 1):
            order = sorted(range(n), key=lambda d: (-abs(d - i), d))
            row = [k] + order
            for s in range(1, n):
                for way in (0, 1):
                    p = i if k == way else n - 1 - i
                    target = min(max(n - s + p, 0), n - 1)
                    row += [order.index(target if k == way else n - 1 - target), int(p < s)]
            p = i if k == 0 else n - 1 - i
            for s in range(n):
                source = (p - s) % n
                row += [source if k == 0 else n - 1 - source, int(p >= s)]
            table.append(row)
    steps_at, forward_at = 1 + n, 1 + n + 4 * (n - 1)
    spot = jnp.stack([2 * z + odd])

    arrived = [[X], [X]]
    arrived[0].append(along(X, 0))

    X_other, dY_other, rows_other = (exchange(v, "dp", 1) for v in (X, dY, adapter_rows))
    others = (X_other, dY_other, rows_other)
    own = own_adapter(A[0].T, after(B, *others)[0], half)
    gathered = swap(own, "dp", chips)
    arrived[1].append(along(after(X, own), 1))

    first, second, third = list(range(1, n - 1)), [n - 1], [n]
    backs = [backward(spot, table, first, after(dY, own, *others), W, n)]

    def onward(s, k, last):
        cost = LATE if s == n - 1 else SOON if (s, k) == (1, 1) else 10**3
        payload = add_on(spot, table, steps_at + 4 * (s - 1) + 2 * k, after(arrived[k][s], last), backs, cost)
        arrived[k].append(along(payload, k))
        return payload

    last = onward(1, 0, backs[0])
    last = onward(1, 1, last)

    ids = adapter_rows.reshape(1, rows), rows_other.reshape(1, rows)
    Xs, dYs = (X, X_other), (dY, dY_other)
    backs.append(backward(spot, table, second, after(dY, last), W, n))
    gathered = after(gathered, backs[1])
    part = low_parts(spot, adapter_slot, ids, Xs, dYs, gathered, rank, n)
    parts = [part] + [exchange(part, "tensor", k) for k in range(1, n)]

    last = part
    for s in range(2, n):
        last = onward(s, 0, last)
        if s == 2:
            own_back = backward(spot, table, third, after(dY, last), W, n)
            last = own_back
        last = onward(s, 1, last)
        if s == 2:
            parts = [after(p, last) for p in parts]
            mine, term, back_term, send = adapters(spot, adapter_slot, ids, parts, Xs, dYs, gathered, rank)
            arriving = swap(mine, "dp", chips)
            other = exchange(send, "dp", 1)
            last = send

    blocks = [(after(X, last),)] + [(arrived[0][s], arrived[1][n - s]) for s in range(1, n)]
    projected, rest = forward(spot, table, forward_at, n, W, blocks, (term, back_term, other), own_back)
    activation, shrink, expand = finish((arrived[0][n], arrived[1][n]), rest, arriving, rank)
    return projected, activation, shrink.T[None], expand[None]


def solution(mesh):
    return jax.shard_map(
        body,
        mesh=mesh,
        in_specs=(
            P("dp", "tensor"),
            P("dp", "tensor"),
            P(None, "tensor"),
            P("dp", "tensor", None),
            P("dp", None, "tensor"),
            P("dp", None),
            P(),
        ),
        out_specs=(
            P("dp", "tensor"),
            P("dp", "tensor"),
            P("dp", "tensor", None),
            P("dp", None, "tensor"),
        ),
        check_vma=False,
    )
```

```python
import jax
import jax.numpy as jnp
from jax import lax
from jax.experimental import pallas as pl
from jax.experimental.pallas import tpu as pltpu
from jax.sharding import PartitionSpec as P

adapter_scale = 2.0
f32, bf16 = jnp.float32, jnp.bfloat16
HBM = pl.BlockSpec(memory_space=pltpu.HBM)
LATE = 10**12
GRADS = 10**10
BIG = 63
SOON = 10**10


def dot(a, b, ca, cb):
    return lax.dot_general(a, b, (((ca,), (cb,)), ((), ())), preferred_element_type=f32)


def exchange(x, axis, offset):
    size = lax.axis_size(axis)
    return lax.ppermute(x, axis, [(i, i ^ offset) for i in range(size)])


def swap(x, axis, groups):
    return lax.all_to_all(x, axis, 0, 0, axis_index_groups=groups, tiled=True)


def after(x, *earlier):
    return lax.optimization_barrier((x,) + earlier)[0]


def call(kernel, grid, prefetch, ins, outs, shapes, scratch, mib=BIG, cost=10**3):
    return pl.pallas_call(
        kernel,
        grid_spec=pltpu.PrefetchScalarGridSpec(
            num_scalar_prefetch=prefetch, grid=grid, in_specs=ins, out_specs=outs, scratch_shapes=list(scratch)
        ),
        out_shape=shapes,
        cost_estimate=pl.CostEstimate(flops=cost, bytes_accessed=1, transcendentals=0),
        compiler_params=pltpu.CompilerParams(vmem_limit_bytes=mib * 2**20),
    )


def array(*shape):
    return pltpu.HBM(shape, bf16)


def far(*xs):
    return [pltpu.with_memory_space_constraint(x, pltpu.HBM) for x in xs]


def vmem(*shape):
    return pltpu.VMEM(shape, bf16)


def look_up(spot, table, column):
    value = jnp.int32(table[0][column])
    for i, row in enumerate(table[1:], 1):
        value = jnp.where(spot[0] == i, row[column], value)
    return value


def sems(count):
    return pltpu.SemaphoreType.DMA((count,))


def fetch(copies, sem, first=0):
    copies = [pltpu.make_async_copy(a, b, sem.at[first + i]) for i, (a, b) in enumerate(copies)]
    for c in copies:
        c.start()
    return copies


def wait(copies):
    for c in copies:
        c.wait()


def own_adapter(A, B, half):
    rank, width = B.shape

    def kernel(A, B, out, both, sem):
        outs = []
        for k, c in enumerate(fetch([(A, both.at[pl.ds(0, rank)]), (B, both.at[pl.ds(rank, rank)])], sem)):
            c.wait()
            span = pl.ds(k * rank, rank)
            outs += fetch([(both.at[span], out.at[j, span]) for j in range(half)], sem, 2 + k * half)
        wait(outs)

    return call(
        kernel, (1,), 0, [HBM, HBM], HBM, array(half, 2 * rank, width), [vmem(2 * rank, width), sems(2 + 2 * half)], mib=4
    )(*far(A, B))


class Stream:
    def __init__(self, W, w, starts, size, sem):
        chunk = size // 4 if size % 512 == 0 else size
        self.copies, self.started, self.done = [], 0, 0
        for b, start in enumerate(starts):
            for i in range(size // chunk):
                source = W.at[pl.ds(pl.multiple_of(start * size + i * chunk, chunk), chunk)]
                k = len(self.copies)
                self.copies.append(pltpu.make_async_copy(source, w.at[pl.ds(b * size + i * chunk, chunk)], sem.at[k]))

    def start(self, count):
        for c in self.copies[self.started : self.started + count]:
            c.start()
        self.started += count

    def take(self, parts):
        for _ in range(len(self.copies) // parts):
            self.copies[self.done].wait()
            self.done += 1
            self.start(1)


def backward_blocks(y, w, done, out, stream, size, coarse, sem):
    blocks = done.shape[0]
    tile = size // coarse
    outs = []
    for b in range(blocks):
        for i in range(coarse):
            stream.take(blocks * coarse)
            span = pl.ds(i * tile, tile)
            done[b, :, span] = dot(y, w[pl.ds(b * size + i * tile, tile)], 1, 1).astype(bf16)
            outs += fetch([(done.at[b, :, span], out.at[b, :, span])], sem, b * coarse + i)
    return outs


def backward(spot, table, columns, dY, W, n):
    rows, width = dY.shape
    size = W.shape[0] // n
    blocks = len(columns)
    coarse = 1 if size % 512 else 2 if blocks > 1 else 4

    def kernel(spot, dY, W, out, y, w, done, sem, out_sem, y_sem):
        ready = fetch([(dY, y)], y_sem)
        ins = Stream(W, w, [look_up(spot, table, c) for c in columns], size, sem)
        ins.start(4 if blocks > 1 else 2)
        wait(ready)
        wait(backward_blocks(y[...], w, done, out, ins, size, coarse, out_sem))

    return call(
        kernel,
        (1,),
        1,
        [HBM, HBM],
        HBM,
        array(blocks, rows, size),
        [vmem(rows, width), vmem(blocks * size, width), vmem(blocks, rows, size), sems(4 * blocks), sems(4 * blocks), sems(1)],
    )(spot, *far(dY, W))


def add_on(spot, table, at, arrived, backs, cost):
    rows, width = arrived.shape
    steps = 2
    size = rows // steps
    count = backs[0].shape[0]

    def kernel(spot, arrived, *refs):
        backs, (out, a, b, sem) = refs[:-4], refs[-4:]
        parts = [pl.ds(i * size, size) for i in range(steps)]
        add, block = look_up(spot, table, at + 1) == 1, look_up(spot, table, at)
        ins = [pltpu.make_async_copy(arrived.at[p], a.at[p], sem.at[i]) for i, p in enumerate(parts)]
        adds = [
            [pltpu.make_async_copy(r.at[lax.rem(block, count), p], b.at[p], sem.at[steps + i]) for r in backs]
            for i, p in enumerate(parts)
        ]
        outs = [pltpu.make_async_copy(a.at[p], out.at[p], sem.at[2 * steps + i]) for i, p in enumerate(parts)]
        for i in range(steps):
            ins[i].start()
            for k in range(len(backs)):
                pl.when(add & (lax.div(block, count) == k))(adds[i][k].start)
        for i, p in enumerate(parts):
            ins[i].wait()

            @pl.when(add)
            def _():
                adds[i][0].wait()
                a[p] = (a[p].astype(f32) + b[p].astype(f32)).astype(bf16)

            outs[i].start()
        wait(outs)

    return call(
        kernel,
        (1,),
        1,
        [HBM] * (1 + len(backs)),
        HBM,
        array(rows, width),
        [vmem(rows, width), vmem(rows, width), sems(3 * steps)],
        mib=8,
        cost=cost,
    )(spot, *far(arrived, *backs))


def finish(arrived, rest):
    rows, width = rest.shape
    steps = 4
    size = rows // steps

    def kernel(one, two, rest, out, held, done, sem):
        refs = [one, two, rest]
        spans = [pl.ds(i * size, size) for i in range(steps)]
        ins = [
            fetch([(r.at[p], held.at[k, p]) for k, r in enumerate(refs)], sem, i * len(refs))
            for i, p in enumerate(spans)
        ]
        outs = []
        for i, p in enumerate(spans):
            wait(ins[i])
            done[p] = (held[0, p].astype(f32) + held[1, p].astype(f32) + held[2, p].astype(f32)).astype(bf16)
            outs += fetch([(done.at[p], out.at[p])], sem, steps * len(refs) + i)
        wait(outs)

    return call(
        kernel,
        (1,),
        0,
        [HBM] * 3,
        HBM,
        array(rows, width),
        [vmem(3, rows, width), vmem(rows, width), sems(4 * steps)],
        mib=16,
    )(*far(*arrived, rest))


def add_up(blocks, rank):
    half, _, width = blocks.shape

    def kernel(blocks, shrink, expand, parts, total, sem):
        wait(fetch([(blocks, parts)], sem))
        total[...] = sum(parts[j].astype(f32) for j in range(half)).astype(bf16)
        wait(fetch([(total.at[pl.ds(0, rank)], shrink), (total.at[pl.ds(rank, rank)], expand)], sem, 1))

    return call(
        kernel,
        (1,),
        0,
        [HBM],
        [HBM] * 2,
        [array(rank, width)] * 2,
        [vmem(*blocks.shape), vmem(2 * rank, width), sems(3)],
        mib=16,
    )(*far(blocks))


def forward(spot, table, at, n, W, blocks, terms, back):
    rows, width = blocks[0][0].shape
    columns = W.shape[1]
    coarse = 2 if width % 512 == 0 else 1
    tile = width // coarse
    count = len(blocks)
    arrays = [b for block in blocks for b in block]

    def kernel(spot, *refs):
        flat, (W, term, back_term, other, back) = refs[: len(arrays)], refs[len(arrays) : len(arrays) + 5]
        out, rest, held, w, total, sides, sem, side_sem = refs[len(arrays) + 5 :]
        flat = iter(flat)
        mine = [[next(flat) for _ in block] for block in blocks]
        lefts = []
        for s, block in enumerate(mine):
            pick = [pltpu.make_async_copy(ref, held.at[s], side_sem.at[s]) for ref in block]
            if len(block) == 1:
                pick[0].start()
            else:
                one = look_up(spot, table, at + 2 * s + 1) == 1
                pl.when(one)(pick[0].start)
                pl.when(jnp.logical_not(one))(pick[1].start)
            lefts.append(pick[0])
        ins = Stream(W, w, [look_up(spot, table, at + 2 * s) for s in range(count)], width, sem)
        ins.start(6)
        own, theirs = pl.ds(0, rows), pl.ds(rows, rows)
        pairs = [term, other.at[own], back_term, other.at[theirs], back.at[back.shape[0] - 1]]
        for s in range(count):
            lefts[s].wait()
            for i in range(coarse):
                k = s * coarse + i
                ins.take(count * coarse)
                if k == count * coarse // 2:
                    added = fetch([(r, sides.at[i]) for i, r in enumerate(pairs)], side_sem, count)
                product = dot(held[s, :, pl.ds(i * tile, tile)], w[pl.ds(s * width + i * tile, tile)], 1, 0)
                if k == 0:
                    total[...] = product
                else:
                    total[...] += product
        wait(added)
        sides[0] = (total[...] + (sides[0].astype(f32) + sides[1].astype(f32))).astype(bf16)
        outs = fetch([(sides.at[0], out)], side_sem, count + 5)
        sides[2] = (sides[2].astype(f32) + sides[3].astype(f32) + sides[4].astype(f32)).astype(bf16)
        wait(outs + fetch([(sides.at[2], rest)], side_sem, count + 6))

    return call(
        kernel,
        (1,),
        1,
        [HBM] * (len(arrays) + 5),
        [HBM] * 2,
        [array(rows, columns), array(rows, width)],
        [
            vmem(count, rows, width),
            vmem(count * width, columns),
            pltpu.VMEM((rows, columns), f32),
            vmem(5, rows, columns),
            sems(4 * count),
            sems(count + 7),
        ],
    )(spot, *far(*arrays, W, *terms, back))


def chosen_of(spot, slots, ids, rank, half):
    ids = jnp.concatenate([r[...] for r in ids], axis=1)
    slot = jnp.zeros(ids.shape, jnp.int32)
    for a in range(slots.shape[0]):
        slot = jnp.where(ids == a, slots[a], slot)
    column = lax.broadcasted_iota(jnp.int32, (half * rank, ids.shape[1]), 0) // rank
    return jnp.where(slot == 2 * column + lax.rem(spot[0], 2), 1.0, 0.0).T > 0.5


def pieces(gathered, downs, ups, rank):
    half = gathered.shape[0]
    return [(gathered.at[j, pl.ds(0, rank)], downs.at[pl.ds(j * rank, rank)]) for j in range(half)] + [
        (gathered.at[j, pl.ds(rank, rank)], ups.at[pl.ds(j * rank, rank)]) for j in range(half)
    ]


def rows_of(X, dY, x, y, rows):
    top, bottom = pl.ds(0, rows), pl.ds(rows, rows)
    return [(X[0], x.at[top]), (X[1], x.at[bottom]), (dY[0], y.at[top]), (dY[1], y.at[bottom])]


def ids_spec(rows):
    return pl.BlockSpec((1, rows), lambda i, *_: (0, 0))


def low_parts(spot, slots, ids, Xs, dYs, gathered, rank, n):
    rows, width = Xs[0].shape
    half = gathered.shape[0]

    def kernel(spot, slots, id0, id1, X, X_other, dY, dY_other, gathered, out, x, y, downs, ups, part, sem):
        rights = pieces(gathered, downs, ups, rank)
        lefts = rows_of((X, X_other), (dY, dY_other), x, y, rows)
        ready = fetch(lefts[:2] + rights[:half], sem)
        more = fetch(lefts[2:] + rights[half:], sem, 2 + half)
        chosen = chosen_of(spot, slots, (id0, id1), rank, half)

        def pick(a, b):
            both = jnp.where(chosen, dot(a[...], b[...], 1, 1), 0)
            return sum(both[:, j * rank : (j + 1) * rank] for j in range(half))

        wait(ready)
        low = pick(x, downs)
        wait(more)
        part[...] = jnp.concatenate([low, pick(y, ups)], axis=1).astype(bf16)
        wait(fetch([(part, out)], sem, 4 + 2 * half))

    return call(
        kernel,
        (1,),
        2,
        [ids_spec(rows)] * 2 + [HBM] * 5,
        HBM,
        array(2 * rows, 2 * rank),
        [vmem(2 * rows, width)] * 2
        + [vmem(half * rank, width)] * 2
        + [vmem(2 * rows, 2 * rank), sems(4 + 2 * half + n)],
    )(spot, slots, *ids, *far(*Xs, *dYs, gathered))


def adapters(spot, slots, ids, few, Xs, dYs, gathered, rank):
    rows, width = Xs[0].shape
    half = gathered.shape[0]

    def kernel(spot, slots, id0, id1, *refs):
        parts, (X, X_other, dY, dY_other, gathered, out, term, back, other, *scratch) = refs[: len(few)], refs[len(few) :]
        x, y, downs, ups, grads, terms, sem, out_sem = scratch
        ins = fetch(
            rows_of((X, X_other), (dY, dY_other), x, y, rows) + pieces(gathered, downs, ups, rank), sem
        )
        chosen = chosen_of(spot, slots, (id0, id1), rank, half)
        total = sum(p[...].astype(f32) for p in parts)
        low, grad = total[:, :rank].astype(bf16), (adapter_scale * total[:, rank:]).astype(bf16)
        zero = jnp.zeros((), bf16)
        low, grad = [jnp.where(chosen, jnp.concatenate([v] * half, axis=1), zero) for v in (low, grad)]
        wait(ins[:2])
        shrink = dot(grad, x[...], 0, 0).astype(bf16)
        for j in range(half):
            grads[j, :rank] = shrink[j * rank : (j + 1) * rank]
        wait(ins[2:4])
        expand = (adapter_scale * dot(low, y[...], 0, 0)).astype(bf16)
        for j in range(half):
            grads[j, rank:] = expand[j * rank : (j + 1) * rank]
        outs = fetch([(grads, out)], out_sem)
        wait(ins[4:])
        top, bottom = pl.ds(0, rows), pl.ds(rows, rows)
        terms[0] = (adapter_scale * dot(low, ups[...], 1, 0)).astype(bf16)
        outs += fetch([(terms.at[0, top], term), (terms.at[0, bottom], other.at[top])], out_sem, 1)
        terms[1] = dot(grad, downs[...], 1, 0).astype(bf16)
        outs += fetch([(terms.at[1, top], back), (terms.at[1, bottom], other.at[bottom])], out_sem, 3)
        wait(outs)

    return call(
        kernel,
        (1,),
        2,
        [ids_spec(rows)] * 2 + [pl.BlockSpec(memory_space=pltpu.VMEM)] * len(few) + [HBM] * 5,
        [HBM] * 4,
        [array(half, 2 * rank, width), array(rows, width), array(rows, width), array(2 * rows, width)],
        [vmem(2 * rows, width)] * 2
        + [vmem(half * rank, width)] * 2
        + [vmem(half, 2 * rank, width), vmem(2, 2 * rows, width), sems(4 + 2 * half), sems(5)],
        mib=60,
        cost=GRADS,
    )(spot, slots, *ids, *[pltpu.with_memory_space_constraint(p, pltpu.VMEM) for p in few], *far(*Xs, *dYs, gathered))


def body(X, dY, W, A, B, adapter_rows, adapter_slot):
    rows, width = X.shape
    rank = A.shape[2]
    n, D = lax.axis_size("tensor"), lax.axis_size("dp")
    z, me = lax.axis_index("tensor"), lax.axis_index("dp")
    half = D // 2
    chips = [list(range(k, D, 2)) for k in (0, 1)]

    odd = me & 1
    up = [(d * n + i, d * n + i + 1) for d in range(D) for i in range(n - 1)]
    pairs = [[(a, b) if (a // n) % 2 == k else (b, a) for a, b in up] for k in (0, 1)]

    def along(x, k):
        return lax.ppermute(x, ("dp", "tensor"), pairs[k])

    table = []
    for i in range(n):
        for k in (0, 1):
            order = sorted(range(n), key=lambda d: (-abs(d - i), d))
            row = [k] + order
            for s in range(1, n):
                for way in (0, 1):
                    p = i if k == way else n - 1 - i
                    target = min(max(n - s + p, 0), n - 1)
                    row += [order.index(target if k == way else n - 1 - target), int(p < s)]
            p = i if k == 0 else n - 1 - i
            for s in range(n):
                source = (p - s) % n
                row += [source if k == 0 else n - 1 - source, int(p >= s)]
            table.append(row)
    steps_at, forward_at = 1 + n, 1 + n + 4 * (n - 1)
    spot = jnp.stack([2 * z + odd])

    arrived = [[X], [X]]
    arrived[0].append(along(X, 0))

    X_other, dY_other, rows_other = (exchange(v, "dp", 1) for v in (X, dY, adapter_rows))
    others = (X_other, dY_other, rows_other)
    own = own_adapter(A[0].T, after(B, *others)[0], half)
    gathered = swap(own, "dp", chips)
    arrived[1].append(along(after(X, own), 1))

    first, second, third = list(range(1, n - 1)), [n - 1], [n]
    backs = [backward(spot, table, first, after(dY, own, *others), W, n)]

    def onward(s, k, last):
        cost = LATE if s == n - 1 else SOON if (s, k) == (1, 1) else 10**3
        payload = add_on(spot, table, steps_at + 4 * (s - 1) + 2 * k, after(arrived[k][s], last), backs, cost)
        arrived[k].append(along(payload, k))
        return payload

    last = onward(1, 0, backs[0])
    last = onward(1, 1, last)

    ids = adapter_rows.reshape(1, rows), rows_other.reshape(1, rows)
    Xs, dYs = (X, X_other), (dY, dY_other)
    backs.append(backward(spot, table, second, after(dY, last), W, n))
    gathered = after(gathered, backs[1])
    part = low_parts(spot, adapter_slot, ids, Xs, dYs, gathered, rank, n)
    parts = [part] + [exchange(part, "tensor", k) for k in range(1, n)]

    last = part
    for s in range(2, n):
        last = onward(s, 0, last)
        if s == 2:
            own_back = backward(spot, table, third, after(dY, last), W, n)
            last = own_back
        last = onward(s, 1, last)
        if s == 2:
            parts = [after(p, last) for p in parts]
            mine, term, back_term, send = adapters(spot, adapter_slot, ids, parts, Xs, dYs, gathered, rank)
            arriving = swap(mine, "dp", chips)
            other = exchange(send, "dp", 1)
            last = send

    blocks = [(after(X, last),)] + [(arrived[0][s], arrived[1][n - s]) for s in range(1, n)]
    projected, rest = forward(spot, table, forward_at, n, W, blocks, (term, back_term, other), own_back)
    shrink, expand = add_up(after(arriving, projected), rank)
    activation = finish((arrived[0][n], arrived[1][n]), after(rest, shrink))
    return projected, activation, shrink.T[None], expand[None]


def solution(mesh):
    return jax.shard_map(
        body,
        mesh=mesh,
        in_specs=(
            P("dp", "tensor"),
            P("dp", "tensor"),
            P(None, "tensor"),
            P("dp", "tensor", None),
            P("dp", None, "tensor"),
            P("dp", None),
            P(),
        ),
        out_specs=(
            P("dp", "tensor"),
            P("dp", "tensor"),
            P("dp", "tensor", None),
            P("dp", None, "tensor"),
        ),
        check_vma=False,
    )
```
